32 devices in a mesh: tm: 4 (over y, x), space: 8 (over z, core).
Axes of the slice: x: 2, y: 2, z: 4, core: 2. Of those that a mesh axis runs over, the one named last changes fastest.
Arguments:
- guess: float32 [8, 3, 96, 64, 128], P('tm', None, 'space'), may hold values from -6 to 6
- source: float32 [8, 3, 96, 64, 128], P('tm', None, 'space'), may hold values from -6 to 6
- regions: int32 [96, 64, 128], P('space'), may hold values from 0 to 3
- conductance: float32 [4], replicated, may hold values from 8 to 32
- reluct: float32 [4], replicated, may hold values from 0.25 to 2
Outputs:
- field: float32 [8, 3, 96, 64, 128], P('tm', None, 'space')
- coarse_residual: float32 [4, 3, 96, 64, 128], P('tm', None, 'space')
The draws below stay inside these ranges and needn't reach their ends.
Inputs may be any that keep to these rules, and one draw needn't show every extreme that they name: `regions`: a region id per cell.
All inputs are finite; a program needn't handle non-finite values.
Results may differ from the reference program's by a relative error of at most 0.0001.
Values sent between devices are 32-bit elements; how exact they have to be, the bound alone decides.
A program may use at most 128 MiB of HBM per device.

```python
import math
import jax
import jax.numpy as jnp

NY = 64
NZ = 128
STEPS = 2
PICARD = 2
REGIONS = 4
NX = 96
NT = 8
N_TM = 4


def set_ends(result, rng, smallest, top_value):
    extent = result.shape
    place = [jax.random.randint(jax.random.fold_in(rng, axis), (), 0, extent[axis]) for axis in range(len(extent))]
    result = result.at[tuple(place)].set(smallest)
    longest = extent.index(max(extent))
    place[longest] = (place[longest] + 1) % extent[longest]
    return result.at[tuple(place)].set(top_value)


def block_scale(key, dims, split, least, largest):
    factor_of = 1.0
    for dim, parts in split:
        heights = jax.random.uniform(jax.random.fold_in(jax.random.fold_in(key, 6), dim), (parts,), jnp.float32, least / len(split), largest / len(split))
        factor_of = factor_of * jnp.repeat(jnp.exp(heights), dims[dim] // parts).reshape((-1,) + (1,) * (len(dims) - 1 - dim))
    return factor_of


def gaussian(stream_key, shape, spread, reach, cuts=(), held_as=jnp.bfloat16):
    result = spread * jax.random.normal(stream_key, shape, jnp.float32)
    if cuts:
        result = result * block_scale(stream_key, shape, cuts, -0.22, 0.18)
    return jnp.clip(result, -reach, reach).astype(held_as)


def setup_inputs(seed: int = 0) -> dict:
    keys = jax.random.split(jax.random.key(seed), 6)
    guess = gaussian(keys[0], (NT, 3, NX, NY, NZ), 1.0, 6.0, ((0, 4), (2, 8)), jnp.float32)
    source = gaussian(keys[1], (NT, 3, NX, NY, NZ), 1.0, 6.0, ((0, 4), (2, 8)), jnp.float32)
    regions = set_ends(jax.random.randint(keys[2], (NX, NY, NZ), 0, REGIONS), jax.random.fold_in(keys[2], 1), 0, REGIONS - 1).astype(jnp.int32)
    conductance = jnp.clip(jnp.exp(jax.random.uniform(keys[3], (REGIONS,), jnp.float32, math.log(8.0), math.log(32.0))), 8.0, 32.0)
    reluct = jnp.clip(jnp.exp(jax.random.uniform(keys[4], (REGIONS,), jnp.float32, math.log(0.25), math.log(2.0))), 0.25, 2.0)
    return {"guess": guess, "source": source, "regions": regions, "conductance": conductance, "reluct": reluct}


def material(regions, table):
    ids = jnp.arange(table.shape[0]).astype(jnp.int32).reshape(-1, 1, 1, 1)
    return jnp.sum(jnp.where(regions[None] == ids, table.reshape(-1, 1, 1, 1), jnp.float32(0.0)), axis=0)


def neighbour_sum(field):
    widths = [(0, 0)] * (field.ndim - 3) + [(1, 1)] * 3
    padded = jnp.pad(field, widths)
    first = padded[..., 2:, 1:-1, 1:-1] + padded[..., :-2, 1:-1, 1:-1]
    second = padded[..., 1:-1, 2:, 1:-1] + padded[..., 1:-1, :-2, 1:-1]
    third = padded[..., 1:-1, 1:-1, 2:] + padded[..., 1:-1, 1:-1, :-2]
    return (first + second) + third


def advance(old, force, cond, base_nu):
    state = old
    for sweep in range(PICARD):
        square = jnp.sum(state * state, axis=-4)
        nu = base_nu * (1.0 + 0.5 * square / (1.0 + square))
        nu = jnp.expand_dims(nu, -4)
        state = (cond * old + force + nu * neighbour_sum(state)) / (cond + 6.0 * nu)
    return state


def coarse_map(value, cond_coarse, base_nu):
    state = value
    for sweep in range(PICARD):
        state = (cond_coarse * value + base_nu * neighbour_sum(state)) / (cond_coarse + 6.0 * base_nu)
    return state


def reference(guess, source, regions, conductance, reluct):
    cond = material(regions, conductance)
    base_nu = material(regions, reluct)
    shape = (N_TM, STEPS) + guess.shape[1:]
    field_all = guess.reshape(shape)
    force_all = source.reshape(shape)
    points = [field_all[:, i] for i in range(STEPS)]
    forces = [force_all[:, i] for i in range(STEPS)]

    def relax_f(points):
        points = list(points)
        for i in range(1, STEPS):
            points[i] = advance(points[i - 1], forces[i], cond, base_nu)
        return points

    points = relax_f(points)
    points[0] = advance(jnp.roll(points[STEPS - 1], 1, axis=0), forces[0], cond, base_nu)
    points = relax_f(points)
    residual = advance(jnp.roll(points[STEPS - 1], 1, axis=0), forces[0], cond, base_nu) - points[0]
    cond_coarse = cond / STEPS
    correction = jnp.zeros_like(residual)
    for k in range(N_TM):
        correction = coarse_map(jnp.roll(correction, 1, axis=0), cond_coarse, base_nu) + residual
    points[0] = points[0] + correction
    points = relax_f(points)
    field = jnp.stack(points, axis=1).reshape(guess.shape)
    return field, residual
```

```python
import jax
import jax.numpy as jnp
from jax import lax
from jax.experimental import pallas as pl
from jax.experimental.pallas import tpu as pltpu
from jax.sharding import PartitionSpec as P

PICARD = 2
MESH = pl.DeviceIdType.MESH
PAD = 8


def place(index, count):
    if count % 4:
        return index
    odd_pair = lax.rem(lax.div(index, 2), 2)
    return index + odd_pair * (1 - 2 * lax.rem(index, 2))


def neighbour_sum(state, x, layers, r0, rows, halo):
    middle, lanes = pl.ds(PAD + r0, rows), state.shape[-1]
    centre = state[:, pl.ds(x + 1, layers), middle, :]
    first = state[:, pl.ds(x + 2, layers), middle, :] + state[:, pl.ds(x, layers), middle, :]
    above = state[:, pl.ds(x + 1, layers), pl.ds(PAD + r0 - 1, rows), :]
    below = state[:, pl.ds(x + 1, layers), pl.ds(PAD + r0 + 1, rows), :]
    if halo is not None:
        top, bottom, depth = halo
        row = lax.broadcasted_iota(jnp.int32, (rows, lanes), 0)

        def filled(side, values, at):
            return jnp.stack([
                jnp.stack([
                    jnp.where(
                        row == at,
                        jnp.broadcast_to(side[pl.ds(c * depth + x + i, 1), :], (rows, lanes)),
                        values[c, i],
                    )
                    for i in range(layers)
                ])
                for c in range(3)
            ])

        above = filled(top, above, 0)
        below = filled(bottom, below, rows - 1)
    flat = centre.reshape(-1, lanes)
    lane = lax.broadcasted_iota(jnp.int32, flat.shape, 1)
    left = jnp.where(lane == 0, 0.0, pltpu.roll(flat, 1, 1))
    right = jnp.where(lane == lanes - 1, 0.0, pltpu.roll(flat, lanes - 1, 1))
    third = (left + right).reshape(centre.shape)
    return centre, (first + (above + below)) + third


def fine(centre, total, known, cond, nu0):
    s = (centre[0] * centre[0] + centre[1] * centre[1]) + centre[2] * centre[2]
    one = 1.0 + s
    weight = nu0 * (one + 0.5 * s)
    scale = 1.0 / (cond * one + 6.0 * weight)
    return (known * (one * scale)[None]) + (weight * scale)[None] * total


def kernel(
    n_tm, n_space,
    guess, source, regions, conductance, reluct,
    field, residual,
    home, home_force, home_known, home_cond, home_nu,
    state, force0, force1, known, points, res, out0,
    cond, nu0, w_old, w_sum,
    row_out, row_in,
    load_sem, home_send, home_recv, halo_send, halo_recv,
    move_send, move_recv, back_send, back_recv, store_sem,
):
    steps, _, depth, height, lanes = guess.shape
    rows = height // n_tm
    t, s = lax.axis_index("tm"), lax.axis_index("space")
    p = place(t, n_tm)
    lower_x, upper_x = s > 0, s < n_space - 1
    lower_y, upper_y = p > 0, p < n_tm - 1

    def wrap(i):
        return lax.rem(i + n_tm, n_tm)

    def block(index):
        return pl.ds(pl.multiple_of(place(index, n_tm) * rows, 8), rows)

    def home_block(index):
        return pl.ds(pl.multiple_of(place(index, n_tm) * rows + PAD, 8), rows)

    load_guess = pltpu.make_async_copy(
        guess.at[0], home.at[0, :, pl.ds(1, depth), pl.ds(PAD, height), :], load_sem.at[0]
    )
    load_force = pltpu.make_async_copy(source.at[1], home_force, load_sem.at[1])
    load_guess.start()
    load_force.start()

    zero_layer = jnp.zeros((3, height, lanes), jnp.float32)
    for b in range(2):
        home[b, :, 0, pl.ds(PAD, height), :] = zero_layer
        home[b, :, depth + 1, pl.ds(PAD, height), :] = zero_layer
        for r0 in (0, PAD + height):
            home[b, :, :, pl.ds(r0, PAD), :] = jnp.zeros((3, depth + 2, PAD, lanes), jnp.float32)
    for b in range(3):
        for layer in (0, depth + 1):
            state[b, :, :, layer, pl.ds(PAD, rows), :] = jnp.zeros((n_tm, 3, rows, lanes), jnp.float32)
    row_in[...] = jnp.zeros_like(row_in)

    barrier = pltpu.get_barrier_semaphore()
    for i in range(1, n_tm):
        pl.semaphore_signal(barrier, inc=1, device_id=(wrap(t + i), s), device_id_type=MESH)

    @pl.when(lower_x)
    def _():
        pl.semaphore_signal(barrier, inc=1, device_id=(t, s - 1), device_id_type=MESH)

    @pl.when(upper_x)
    def _():
        pl.semaphore_signal(barrier, inc=1, device_id=(t, s + 1), device_id_type=MESH)

    between = jnp.logical_and(lower_x, upper_x)

    @pl.when(between)
    def _():
        pl.semaphore_wait(barrier, n_tm + 1)

    @pl.when(jnp.logical_not(between))
    def _():
        pl.semaphore_wait(barrier, n_tm)

    def home_copies(b, first=None, last=None):
        view = pl.ds(PAD, height)
        first = home.at[b, :, 1, view, :] if first is None else first
        last = home.at[b, :, depth, view, :] if last is None else last
        down = pltpu.make_async_remote_copy(
            first, home.at[b, :, depth + 1, view, :], home_send.at[b, 0], home_recv.at[b, 0],
            device_id=(t, s - 1), device_id_type=MESH,
        )
        up = pltpu.make_async_remote_copy(
            last, home.at[b, :, 0, view, :], home_send.at[b, 1], home_recv.at[b, 1],
            device_id=(t, s + 1), device_id_type=MESH,
        )
        return down, up

    def start_pair(copies, low, high):
        @pl.when(low)
        def _():
            copies[0].start()

        @pl.when(high)
        def _():
            copies[1].start()

    def wait_pair(copies, low, high):
        @pl.when(low)
        def _():
            copies[0].wait_send()
            copies[1].wait_recv()

        @pl.when(high)
        def _():
            copies[1].wait_send()
            copies[0].wait_recv()

    def home_edges(b):
        start_pair(home_copies(b), lower_x, upper_x)

    def home_wait(b):
        wait_pair(home_copies(b), lower_x, upper_x)

    first_edges = home_copies(0, guess.at[0, :, 0], guess.at[0, :, depth - 1])
    start_pair(first_edges, lower_x, upper_x)

    def moves(which, src, dst):
        return [
            pltpu.make_async_remote_copy(
                src(wrap(t + i)), dst(t), move_send.at[which, i], move_recv.at[which, t],
                device_id=(wrap(t + i), s), device_id_type=MESH,
            )
            for i in range(1, n_tm)
        ]

    def start_moves(which, src, dst):
        pltpu.make_async_copy(src(t), dst(t), move_recv.at[which, t]).start()
        for copy in moves(which, src, dst):
            copy.start()

    def wait_moves(which, dst, index):
        pltpu.make_async_copy(dst(index), dst(index), move_recv.at[which, index]).wait()

    def source_rows(i):
        return lambda j: source.at[i, :, :, block(j), :]

    def u_rows(j):
        return home.at[2, :, pl.ds(1, depth), home_block(j), :]

    def u_slot(j):
        return state.at[0, wrap(j + 1), :, pl.ds(1, depth), pl.ds(PAD, rows), :]

    def f0_slot(j):
        return force0.at[j]

    def f1_slot(j):
        return force1.at[j]

    start_moves(0, source_rows(0), f0_slot)

    def lookup(ids, table):
        value = jnp.zeros(ids.shape, jnp.float32)
        for i in range(table.shape[0]):
            value = jnp.where(ids == i, table[i], value)
        return value

    my_rows = pl.ds(pl.multiple_of(p * rows, 8), rows)

    @pl.loop(0, depth)
    def _(x):
        ids = regions[x]
        home_cond[x] = lookup(ids, conductance)
        home_nu[x] = lookup(ids, reluct)
        c = home_cond[x, my_rows, :]
        n = home_nu[x, my_rows, :]
        cond[x] = c
        nu0[x] = n
        half = c / steps
        inverse = 1.0 / (half + 6.0 * n)
        w_old[x] = half * inverse
        w_sum[x] = n * inverse

    chunk = 32 if height % 32 == 0 else height

    def home_sweep(b, first):
        @pl.loop(0, depth)
        def _(x):
            for r0 in range(0, height, chunk):
                cut = pl.ds(r0, chunk)
                centre, total = neighbour_sum(home.at[b], x, 1, r0, chunk, None)
                c, n = home_cond[pl.ds(x, 1), cut, :], home_nu[pl.ds(x, 1), cut, :]
                if first:
                    k = c[None] * centre + home_force[:, pl.ds(x, 1), cut, :]
                    home_known[:, pl.ds(x, 1), cut, :] = k
                else:
                    k = home_known[:, pl.ds(x, 1), cut, :]
                home[b + 1, :, pl.ds(x + 1, 1), pl.ds(PAD + r0, chunk), :] = fine(centre, total, k, c, n)

    load_guess.wait()
    load_force.wait()
    wait_pair(first_edges, lower_x, upper_x)
    home_sweep(0, True)
    home_edges(1)
    home_wait(1)
    home_sweep(1, False)
    start_moves(1, u_rows, u_slot)
    start_moves(2, source_rows(1), f1_slot)

    def halo_copies(b, k):
        view = pl.ds(PAD, rows)
        tm_low, tm_high = place(p - 1, n_tm), place(p + 1, n_tm)
        x_down = pltpu.make_async_remote_copy(
            state.at[b, k, :, 1, view, :], state.at[b, k, :, depth + 1, view, :],
            halo_send.at[b, k, 0], halo_recv.at[b, k, 0], device_id=(t, s - 1), device_id_type=MESH,
        )
        x_up = pltpu.make_async_remote_copy(
            state.at[b, k, :, depth, view, :], state.at[b, k, :, 0, view, :],
            halo_send.at[b, k, 1], halo_recv.at[b, k, 1], device_id=(t, s + 1), device_id_type=MESH,
        )
        y_down = pltpu.make_async_remote_copy(
            row_out.at[b, k, 0], row_in.at[b, k, 1],
            halo_send.at[b, k, 2], halo_recv.at[b, k, 2], device_id=(tm_low, s), device_id_type=MESH,
        )
        y_up = pltpu.make_async_remote_copy(
            row_out.at[b, k, 1], row_in.at[b, k, 0],
            halo_send.at[b, k, 3], halo_recv.at[b, k, 3], device_id=(tm_high, s), device_id_type=MESH,
        )
        return (x_down, x_up), (y_down, y_up)

    def send_halo(b, k):
        along_x, along_y = halo_copies(b, k)
        start_pair(along_y, lower_y, upper_y)
        start_pair(along_x, lower_x, upper_x)

    def wait_halo(b, k):
        along_x, along_y = halo_copies(b, k)
        wait_pair(along_y, lower_y, upper_y)
        wait_pair(along_x, lower_x, upper_x)

    layers = 2 if depth % 2 == 0 else 1

    def keep_rows(b, k, x, values):
        for c in range(3):
            for i in range(layers):
                row_out[b, k, 0, pl.ds(c * depth + x + i, 1), :] = values[c, i, 0:1, :]
                row_out[b, k, 1, pl.ds(c * depth + x + i, 1), :] = values[c, i, rows - 1:rows, :]

    def sweep(b, b_out, kind, first, shift, keep):
        @pl.loop(0, n_tm)
        def _(k):
            k_in = wrap(k - 1) if shift else k
            wait_halo(b, k_in)
            halo = (row_in.at[b, k_in, 0], row_in.at[b, k_in, 1], depth)

            @pl.loop(0, depth // layers)
            def _(step):
                x = step * layers
                cut = pl.ds(x, layers)
                centre, total = neighbour_sum(state.at[b, k_in], x, layers, 0, rows, halo)
                if kind == "coarse":
                    k_now = w_old[cut][None] * centre if first else known[k, :, cut]
                    value = k_now + w_sum[cut][None] * total
                else:
                    c, n = cond[cut], nu0[cut]
                    forces = force0 if kind == "force0" else force1
                    k_now = c[None] * centre + forces[k, :, cut] if first else known[k, :, cut]
                    value = fine(centre, total, k_now, c, n)
                if first:
                    known[k, :, cut] = k_now
                if keep == "points":
                    points[k, :, cut] = value
                elif keep == "residual":
                    value = value - points[k, :, cut]
                    res[k, :, cut] = value
                elif keep == "correction":
                    value = value + res[k, :, cut]
                elif keep == "final":
                    out0[k, :, cut] = points[k, :, cut] + (value + res[k, :, cut])
                if keep != "final":
                    state[b_out, k, :, pl.ds(x + 1, layers), pl.ds(PAD, rows), :] = value
                    keep_rows(b_out, k, x, value)

            if keep != "final":
                send_halo(b_out, k)
            if keep == "residual":
                send_back(0, k)
            if keep == "final":
                send_back(1, k)

    def back_view(which, index):
        if which == 0:
            return residual.at[0, :, :, block(index), :]
        return home.at[0, :, pl.ds(1, depth), home_block(index), :]

    def back_source(which, k):
        return res.at[k] if which == 0 else out0.at[k]

    def back_copy(which, k):
        return pltpu.make_async_remote_copy(
            back_source(which, k), back_view(which, t), back_send.at[which, k], back_recv.at[which, t],
            device_id=(k, s), device_id_type=MESH,
        )

    def send_back(which, k):
        @pl.when(k == t)
        def _():
            pltpu.make_async_copy(back_source(which, k), back_view(which, t), back_recv.at[which, t]).start()

        @pl.when(k != t)
        def _():
            back_copy(which, k).start()

    def wait_back(which):
        for i in range(n_tm):
            j = wrap(t + i)
            view = back_view(which, j)
            pltpu.make_async_copy(view, view, back_recv.at[which, j]).wait()
            if i:
                back_copy(which, j).wait_send()

    for i in range(n_tm):
        j = wrap(t - i)
        slot = wrap(j + 1)
        wait_moves(1, u_slot, j)

        @pl.loop(0, depth // layers)
        def _(step):
            x = step * layers
            keep_rows(0, slot, x, state[0, slot, :, pl.ds(x + 1, layers), pl.ds(PAD, rows), :])

        send_halo(0, slot)

    for j in range(n_tm):
        wait_moves(0, f0_slot, j)
    sweep(0, 1, "force0", True, False, None)
    sweep(1, 2, "force0", False, False, "points")
    for j in range(n_tm):
        wait_moves(2, f1_slot, j)
    sweep(2, 0, "force1", True, False, None)
    sweep(0, 1, "force1", False, False, None)
    sweep(1, 2, "force0", True, True, None)
    sweep(2, 0, "force0", False, False, "residual")
    b = 0
    for k in range(1, n_tm):
        sweep(b, (b + 1) % 3, "coarse", True, True, None)
        sweep((b + 1) % 3, (b + 2) % 3, "coarse", False, False, "final" if k == n_tm - 1 else "correction")
        b = (b + 2) % 3

    for copy in moves(0, source_rows(0), f0_slot):
        copy.wait_send()
    for copy in moves(1, u_rows, u_slot):
        copy.wait_send()
    for copy in moves(2, source_rows(1), f1_slot):
        copy.wait_send()

    wait_back(1)
    home_edges(0)
    store0 = pltpu.make_async_copy(
        home.at[0, :, pl.ds(1, depth), pl.ds(PAD, height), :], field.at[0], store_sem.at[0]
    )
    store0.start()
    home_wait(0)
    home_sweep(0, True)
    home_edges(1)
    home_wait(1)
    home_sweep(1, False)
    store1 = pltpu.make_async_copy(
        home.at[2, :, pl.ds(1, depth), pl.ds(PAD, height), :], field.at[1], store_sem.at[1]
    )
    store1.start()
    wait_back(0)
    store0.wait()
    store1.wait()


def solution(mesh):
    n_tm, n_space = mesh.shape["tm"], mesh.shape["space"]

    def body(guess, source, regions, conductance, reluct):
        steps, comps, depth, height, lanes = guess.shape
        rows = height // n_tm
        edge_rows = -(-comps * depth // 8) * 8
        f32 = jnp.float32
        whole = (n_tm, comps, depth, rows, lanes)

        def call(*args):
            return kernel(n_tm, n_space, *args)

        return pl.pallas_call(
            call,
            out_shape=(
                jax.ShapeDtypeStruct(guess.shape, f32),
                jax.ShapeDtypeStruct((1,) + guess.shape[1:], f32),
            ),
            in_specs=[
                pl.BlockSpec(memory_space=pl.ANY),
                pl.BlockSpec(memory_space=pl.ANY),
                pl.BlockSpec(memory_space=pltpu.VMEM),
                pl.BlockSpec(memory_space=pltpu.SMEM),
                pl.BlockSpec(memory_space=pltpu.SMEM),
            ],
            out_specs=(pl.BlockSpec(memory_space=pl.ANY), pl.BlockSpec(memory_space=pl.ANY)),
            scratch_shapes=[
                pltpu.VMEM((3, comps, depth + 2, height + 2 * PAD, lanes), f32),
                pltpu.VMEM((comps, depth, height, lanes), f32),
                pltpu.VMEM((comps, depth, height, lanes), f32),
                pltpu.VMEM((depth, height, lanes), f32),
                pltpu.VMEM((depth, height, lanes), f32),
                pltpu.VMEM((3, n_tm, comps, depth + 2, rows + 2 * PAD, lanes), f32),
                pltpu.VMEM(whole, f32),
                pltpu.VMEM(whole, f32),
                pltpu.VMEM(whole, f32),
                pltpu.VMEM(whole, f32),
                pltpu.VMEM(whole, f32),
                pltpu.VMEM(whole, f32),
                pltpu.VMEM((depth, rows, lanes), f32),
                pltpu.VMEM((depth, rows, lanes), f32),
                pltpu.VMEM((depth, rows, lanes), f32),
                pltpu.VMEM((depth, rows, lanes), f32),
                pltpu.VMEM((3, n_tm, 2, edge_rows, lanes), f32),
                pltpu.VMEM((3, n_tm, 2, edge_rows, lanes), f32),
                pltpu.SemaphoreType.DMA((2,)),
                pltpu.SemaphoreType.DMA((2, 2)),
                pltpu.SemaphoreType.DMA((2, 2)),
                pltpu.SemaphoreType.DMA((3, n_tm, 4)),
                pltpu.SemaphoreType.DMA((3, n_tm, 4)),
                pltpu.SemaphoreType.DMA((3, n_tm)),
                pltpu.SemaphoreType.DMA((3, n_tm)),
                pltpu.SemaphoreType.DMA((2, n_tm)),
                pltpu.SemaphoreType.DMA((2, n_tm)),
                pltpu.SemaphoreType.DMA((2,)),
            ],
            compiler_params=pltpu.CompilerParams(
                collective_id=0, has_side_effects=True, vmem_limit_bytes=48 * 1024 * 1024
            ),
        )(guess, source, regions, conductance, reluct)

    in_specs = (
        P("tm", None, "space", None, None),
        P("tm", None, "space", None, None),
        P("space", None, None),
        P(),
        P(),
    )
    out_specs = (P("tm", None, "space", None, None), P("tm", None, "space", None, None))
    return jax.shard_map(body, mesh=mesh, in_specs=in_specs, out_specs=out_specs, check_vma=False)
```

```python
import jax
import jax.numpy as jnp
from jax import lax
from jax.experimental import pallas as pl
from jax.experimental.pallas import tpu as pltpu
from jax.sharding import PartitionSpec as P

PICARD = 2
MESH = pl.DeviceIdType.MESH
PAD = 8


def place(index, count):
    if count % 4:
        return index
    odd_pair = lax.rem(lax.div(index, 2), 2)
    return index + odd_pair * (1 - 2 * lax.rem(index, 2))


def neighbour_sum(state, x, layers, r0, rows, halo):
    middle, lanes = pl.ds(PAD + r0, rows), state.shape[-1]
    centre = state[:, pl.ds(x + 1, layers), middle, :]
    first = state[:, pl.ds(x + 2, layers), middle, :] + state[:, pl.ds(x, layers), middle, :]
    above = state[:, pl.ds(x + 1, layers), pl.ds(PAD + r0 - 1, rows), :]
    below = state[:, pl.ds(x + 1, layers), pl.ds(PAD + r0 + 1, rows), :]
    if halo is not None:
        top, bottom, depth = halo
        row = lax.broadcasted_iota(jnp.int32, (rows, lanes), 0)

        def filled(side, values, at):
            return jnp.stack([
                jnp.stack([
                    jnp.where(
                        row == at,
                        jnp.broadcast_to(side[pl.ds(c * depth + x + i, 1), :], (rows, lanes)),
                        values[c, i],
                    )
                    for i in range(layers)
                ])
                for c in range(3)
            ])

        above = filled(top, above, 0)
        below = filled(bottom, below, rows - 1)
    flat = centre.reshape(-1, lanes)
    lane = lax.broadcasted_iota(jnp.int32, flat.shape, 1)
    left = jnp.where(lane == 0, 0.0, pltpu.roll(flat, 1, 1))
    right = jnp.where(lane == lanes - 1, 0.0, pltpu.roll(flat, lanes - 1, 1))
    third = (left + right).reshape(centre.shape)
    return centre, (first + (above + below)) + third


def fine(centre, total, known, cond, nu0):
    s = (centre[0] * centre[0] + centre[1] * centre[1]) + centre[2] * centre[2]
    one = 1.0 + s
    weight = nu0 * (one + 0.5 * s)
    below = cond * one + 6.0 * weight
    scale = pl.reciprocal(below, approx=True)
    scale = scale * (2.0 - below * scale)
    return (known * (one * scale)[None]) + (weight * scale)[None] * total


def kernel(
    n_tm, n_space,
    guess, source, regions, conductance, reluct,
    field, residual,
    home0, home1, home2, home_force, home_known, home_cond, home_nu,
    state0, state1, state2, force0, force1, known, points, res, out0,
    cond, nu0, w_old, w_sum,
    row_out, row_in,
    load_sem, home_send, home_recv, halo_send, halo_recv,
    move_send, move_recv, back_send, back_recv, store_sem,
):
    steps, _, depth, height, lanes = guess.shape
    rows = height // n_tm
    home, state = (home0, home1, home2), (state0, state1, state2)
    t, s = lax.axis_index("tm"), lax.axis_index("space")
    p = place(t, n_tm)
    lower_x, upper_x = s > 0, s < n_space - 1
    lower_y, upper_y = p > 0, p < n_tm - 1

    def wrap(i):
        return lax.rem(i + n_tm, n_tm)

    def block(index):
        return pl.ds(pl.multiple_of(place(index, n_tm) * rows, 8), rows)

    def home_block(index):
        return pl.ds(pl.multiple_of(place(index, n_tm) * rows + PAD, 8), rows)

    load_guess = pltpu.make_async_copy(
        guess.at[0], home[0].at[:, pl.ds(1, depth), pl.ds(PAD, height), :], load_sem.at[0]
    )
    load_force = pltpu.make_async_copy(source.at[1], home_force, load_sem.at[1])
    load_guess.start()
    load_force.start()

    zero_layer = jnp.zeros((3, height, lanes), jnp.float32)
    for b in range(2):
        home[b][:, 0, pl.ds(PAD, height), :] = zero_layer
        home[b][:, depth + 1, pl.ds(PAD, height), :] = zero_layer
        for r0 in (0, PAD + height):
            home[b][:, :, pl.ds(r0, PAD), :] = jnp.zeros((3, depth + 2, PAD, lanes), jnp.float32)
    for b in range(3):
        for layer in (0, depth + 1):
            state[b][:, :, layer, pl.ds(PAD, rows), :] = jnp.zeros((n_tm, 3, rows, lanes), jnp.float32)
    row_in[...] = jnp.zeros_like(row_in)

    barrier = pltpu.get_barrier_semaphore()
    for i in range(1, n_tm):
        pl.semaphore_signal(barrier, inc=1, device_id=(wrap(t + i), s), device_id_type=MESH)

    @pl.when(lower_x)
    def _():
        pl.semaphore_signal(barrier, inc=1, device_id=(t, s - 1), device_id_type=MESH)

    @pl.when(upper_x)
    def _():
        pl.semaphore_signal(barrier, inc=1, device_id=(t, s + 1), device_id_type=MESH)

    between = jnp.logical_and(lower_x, upper_x)

    @pl.when(between)
    def _():
        pl.semaphore_wait(barrier, n_tm + 1)

    @pl.when(jnp.logical_not(between))
    def _():
        pl.semaphore_wait(barrier, n_tm)

    def home_copies(b, first=None, last=None):
        view = pl.ds(PAD, height)
        first = home[b].at[:, 1, view, :] if first is None else first
        last = home[b].at[:, depth, view, :] if last is None else last
        down = pltpu.make_async_remote_copy(
            first, home[b].at[:, depth + 1, view, :], home_send.at[b, 0], home_recv.at[b, 0],
            device_id=(t, s - 1), device_id_type=MESH,
        )
        up = pltpu.make_async_remote_copy(
            last, home[b].at[:, 0, view, :], home_send.at[b, 1], home_recv.at[b, 1],
            device_id=(t, s + 1), device_id_type=MESH,
        )
        return down, up

    def start_pair(copies, low, high):
        @pl.when(low)
        def _():
            copies[0].start()

        @pl.when(high)
        def _():
            copies[1].start()

    def wait_pair(copies, low, high):
        @pl.when(low)
        def _():
            copies[0].wait_send()
            copies[1].wait_recv()

        @pl.when(high)
        def _():
            copies[1].wait_send()
            copies[0].wait_recv()

    def home_edges(b):
        start_pair(home_copies(b), lower_x, upper_x)

    def home_wait(b):
        wait_pair(home_copies(b), lower_x, upper_x)

    first_edges = home_copies(0, guess.at[0, :, 0], guess.at[0, :, depth - 1])
    start_pair(first_edges, lower_x, upper_x)

    def moves(which, src, dst):
        return [
            pltpu.make_async_remote_copy(
                src(wrap(t + i)), dst(t), move_send.at[which, i], move_recv.at[which, t],
                device_id=(wrap(t + i), s), device_id_type=MESH,
            )
            for i in range(1, n_tm)
        ]

    def start_moves(which, src, dst):
        pltpu.make_async_copy(src(t), dst(t), move_recv.at[which, t]).start()
        for copy in moves(which, src, dst):
            copy.start()

    def wait_moves(which, dst, index):
        pltpu.make_async_copy(dst(index), dst(index), move_recv.at[which, index]).wait()

    def source_rows(i):
        return lambda j: source.at[i, :, :, block(j), :]

    def u_rows(j):
        return home[2].at[:, pl.ds(1, depth), home_block(j), :]

    def u_slot(j):
        return state[0].at[wrap(j + 1), :, pl.ds(1, depth), pl.ds(PAD, rows), :]

    def f0_slot(j):
        return force0.at[j]

    def f1_slot(j):
        return force1.at[j]

    start_moves(0, source_rows(0), f0_slot)

    def lookup(ids, table):
        value = jnp.zeros(ids.shape, jnp.float32)
        for i in range(table.shape[0]):
            value = jnp.where(ids == i, table[i], value)
        return value

    my_rows = pl.ds(pl.multiple_of(p * rows, 8), rows)

    @pl.loop(0, depth)
    def _(x):
        ids = regions[x]
        home_cond[x] = lookup(ids, conductance)
        home_nu[x] = lookup(ids, reluct)
        c = home_cond[x, my_rows, :]
        n = home_nu[x, my_rows, :]
        cond[x] = c
        nu0[x] = n
        half = c / steps
        inverse = 1.0 / (half + 6.0 * n)
        w_old[x] = half * inverse
        w_sum[x] = n * inverse

    chunk = height

    def home_sweep(b, first):
        @pl.loop(0, depth)
        def _(x):
            for r0 in range(0, height, chunk):
                cut = pl.ds(r0, chunk)
                centre, total = neighbour_sum(home[b], x, 1, r0, chunk, None)
                c, n = home_cond[pl.ds(x, 1), cut, :], home_nu[pl.ds(x, 1), cut, :]
                if first:
                    k = c[None] * centre + home_force[:, pl.ds(x, 1), cut, :]
                    home_known[:, pl.ds(x, 1), cut, :] = k
                else:
                    k = home_known[:, pl.ds(x, 1), cut, :]
                home[b + 1][:, pl.ds(x + 1, 1), pl.ds(PAD + r0, chunk), :] = fine(centre, total, k, c, n)

    load_guess.wait()
    load_force.wait()
    wait_pair(first_edges, lower_x, upper_x)
    home_sweep(0, True)
    home_edges(1)
    home_wait(1)
    home_sweep(1, False)
    start_moves(1, u_rows, u_slot)
    start_moves(2, source_rows(1), f1_slot)

    def halo_copies(b, k):
        view = pl.ds(PAD, rows)
        tm_low, tm_high = place(p - 1, n_tm), place(p + 1, n_tm)
        x_down = pltpu.make_async_remote_copy(
            state[b].at[k, :, 1, view, :], state[b].at[k, :, depth + 1, view, :],
            halo_send.at[b, k, 0], halo_recv.at[b, k, 0], device_id=(t, s - 1), device_id_type=MESH,
        )
        x_up = pltpu.make_async_remote_copy(
            state[b].at[k, :, depth, view, :], state[b].at[k, :, 0, view, :],
            halo_send.at[b, k, 1], halo_recv.at[b, k, 1], device_id=(t, s + 1), device_id_type=MESH,
        )
        y_down = pltpu.make_async_remote_copy(
            row_out.at[b, k, 0], row_in.at[b, k, 1],
            halo_send.at[b, k, 2], halo_recv.at[b, k, 2], device_id=(tm_low, s), device_id_type=MESH,
        )
        y_up = pltpu.make_async_remote_copy(
            row_out.at[b, k, 1], row_in.at[b, k, 0],
            halo_send.at[b, k, 3], halo_recv.at[b, k, 3], device_id=(tm_high, s), device_id_type=MESH,
        )
        return (x_down, x_up), (y_down, y_up)

    def send_halo(b, k):
        along_x, along_y = halo_copies(b, k)
        start_pair(along_y, lower_y, upper_y)
        start_pair(along_x, lower_x, upper_x)

    def wait_halo(b, k):
        along_x, along_y = halo_copies(b, k)
        wait_pair(along_y, lower_y, upper_y)
        wait_pair(along_x, lower_x, upper_x)

    layers = 4 if depth % 4 == 0 else 1

    def keep_rows(b, k, x, values):
        for c in range(3):
            for i in range(layers):
                row_out[b, k, 0, pl.ds(c * depth + x + i, 1), :] = values[c, i, 0:1, :]
                row_out[b, k, 1, pl.ds(c * depth + x + i, 1), :] = values[c, i, rows - 1:rows, :]

    def sweep(b, b_out, kind, first, shift, keep):
        @pl.loop(0, n_tm)
        def _(k):
            k_in = wrap(k - 1) if shift else k
            wait_halo(b, k_in)
            halo = (row_in.at[b, k_in, 0], row_in.at[b, k_in, 1], depth)

            @pl.loop(0, depth // layers)
            def _(step):
                x = step * layers
                cut = pl.ds(x, layers)
                centre, total = neighbour_sum(state[b].at[k_in], x, layers, 0, rows, halo)
                if kind == "coarse":
                    k_now = w_old[cut][None] * centre if first else known[k, :, cut]
                    value = k_now + w_sum[cut][None] * total
                else:
                    c, n = cond[cut], nu0[cut]
                    forces = force0 if kind == "force0" else force1
                    k_now = c[None] * centre + forces[k, :, cut] if first else known[k, :, cut]
                    value = fine(centre, total, k_now, c, n)
                if first:
                    known[k, :, cut] = k_now
                if keep == "points":
                    points[k, :, cut] = value
                elif keep == "residual":
                    value = value - points[k, :, cut]
                    res[k, :, cut] = value
                elif keep == "correction":
                    value = value + res[k, :, cut]
                elif keep == "final":
                    out0[k, :, cut] = points[k, :, cut] + (value + res[k, :, cut])
                if keep != "final":
                    state[b_out][k, :, pl.ds(x + 1, layers), pl.ds(PAD, rows), :] = value
                    keep_rows(b_out, k, x, value)

            if keep != "final":
                send_halo(b_out, k)
            if keep == "residual":
                send_back(0, k)
            if keep == "final":
                send_back(1, k)

    def back_view(which, index):
        if which == 0:
            return residual.at[0, :, :, block(index), :]
        return home[0].at[:, pl.ds(1, depth), home_block(index), :]

    def back_source(which, k):
        return res.at[k] if which == 0 else out0.at[k]

    def back_copy(which, k):
        return pltpu.make_async_remote_copy(
            back_source(which, k), back_view(which, t), back_send.at[which, k], back_recv.at[which, t],
            device_id=(k, s), device_id_type=MESH,
        )

    def send_back(which, k):
        @pl.when(k == t)
        def _():
            pltpu.make_async_copy(back_source(which, k), back_view(which, t), back_recv.at[which, t]).start()

        @pl.when(k != t)
        def _():
            back_copy(which, k).start()

    def wait_back(which):
        for i in range(n_tm):
            j = wrap(t + i)
            view = back_view(which, j)
            pltpu.make_async_copy(view, view, back_recv.at[which, j]).wait()
            if i:
                back_copy(which, j).wait_send()

    for i in range(n_tm):
        j = wrap(t - i)
        slot = wrap(j + 1)
        wait_moves(1, u_slot, j)

        @pl.loop(0, depth // layers)
        def _(step):
            x = step * layers
            keep_rows(0, slot, x, state[0][slot, :, pl.ds(x + 1, layers), pl.ds(PAD, rows), :])

        send_halo(0, slot)

    for j in range(n_tm):
        wait_moves(0, f0_slot, j)
    sweep(0, 1, "force0", True, False, None)
    sweep(1, 2, "force0", False, False, "points")
    for j in range(n_tm):
        wait_moves(2, f1_slot, j)
    sweep(2, 0, "force1", True, False, None)
    sweep(0, 1, "force1", False, False, None)
    sweep(1, 2, "force0", True, True, None)
    sweep(2, 0, "force0", False, False, "residual")
    b = 0
    for k in range(1, n_tm):
        sweep(b, (b + 1) % 3, "coarse", True, True, None)
        sweep((b + 1) % 3, (b + 2) % 3, "coarse", False, False, "final" if k == n_tm - 1 else "correction")
        b = (b + 2) % 3

    for copy in moves(0, source_rows(0), f0_slot):
        copy.wait_send()
    for copy in moves(1, u_rows, u_slot):
        copy.wait_send()
    for copy in moves(2, source_rows(1), f1_slot):
        copy.wait_send()

    wait_back(1)
    home_edges(0)
    store0 = pltpu.make_async_copy(
        home[0].at[:, pl.ds(1, depth), pl.ds(PAD, height), :], field.at[0], store_sem.at[0]
    )
    store0.start()
    home_wait(0)
    home_sweep(0, True)
    home_edges(1)
    home_wait(1)
    home_sweep(1, False)
    store1 = pltpu.make_async_copy(
        home[2].at[:, pl.ds(1, depth), pl.ds(PAD, height), :], field.at[1], store_sem.at[1]
    )
    store1.start()
    wait_back(0)
    store0.wait()
    store1.wait()


def solution(mesh):
    n_tm, n_space = mesh.shape["tm"], mesh.shape["space"]

    def body(guess, source, regions, conductance, reluct):
        steps, comps, depth, height, lanes = guess.shape
        rows = height // n_tm
        edge_rows = -(-comps * depth // 8) * 8
        f32 = jnp.float32
        whole = (n_tm, comps, depth, rows, lanes)

        def call(*args):
            return kernel(n_tm, n_space, *args)

        return pl.pallas_call(
            call,
            out_shape=(
                jax.ShapeDtypeStruct(guess.shape, f32),
                jax.ShapeDtypeStruct((1,) + guess.shape[1:], f32),
            ),
            in_specs=[
                pl.BlockSpec(memory_space=pl.ANY),
                pl.BlockSpec(memory_space=pl.ANY),
                pl.BlockSpec(memory_space=pltpu.VMEM),
                pl.BlockSpec(memory_space=pltpu.SMEM),
                pl.BlockSpec(memory_space=pltpu.SMEM),
            ],
            out_specs=(pl.BlockSpec(memory_space=pl.ANY), pl.BlockSpec(memory_space=pl.ANY)),
            scratch_shapes=[
                pltpu.VMEM((comps, depth + 2, height + 2 * PAD, lanes), f32),
                pltpu.VMEM((comps, depth + 2, height + 2 * PAD, lanes), f32),
                pltpu.VMEM((comps, depth + 2, height + 2 * PAD, lanes), f32),
                pltpu.VMEM((comps, depth, height, lanes), f32),
                pltpu.VMEM((comps, depth, height, lanes), f32),
                pltpu.VMEM((depth, height, lanes), f32),
                pltpu.VMEM((depth, height, lanes), f32),
                pltpu.VMEM((n_tm, comps, depth + 2, rows + 2 * PAD, lanes), f32),
                pltpu.VMEM((n_tm, comps, depth + 2, rows + 2 * PAD, lanes), f32),
                pltpu.VMEM((n_tm, comps, depth + 2, rows + 2 * PAD, lanes), f32),
                pltpu.VMEM(whole, f32),
                pltpu.VMEM(whole, f32),
                pltpu.VMEM(whole, f32),
                pltpu.VMEM(whole, f32),
                pltpu.VMEM(whole, f32),
                pltpu.VMEM(whole, f32),
                pltpu.VMEM((depth, rows, lanes), f32),
                pltpu.VMEM((depth, rows, lanes), f32),
                pltpu.VMEM((depth, rows, lanes), f32),
                pltpu.VMEM((depth, rows, lanes), f32),
                pltpu.VMEM((3, n_tm, 2, edge_rows, lanes), f32),
                pltpu.VMEM((3, n_tm, 2, edge_rows, lanes), f32),
                pltpu.SemaphoreType.DMA((2,)),
                pltpu.SemaphoreType.DMA((2, 2)),
                pltpu.SemaphoreType.DMA((2, 2)),
                pltpu.SemaphoreType.DMA((3, n_tm, 4)),
                pltpu.SemaphoreType.DMA((3, n_tm, 4)),
                pltpu.SemaphoreType.DMA((3, n_tm)),
                pltpu.SemaphoreType.DMA((3, n_tm)),
                pltpu.SemaphoreType.DMA((2, n_tm)),
                pltpu.SemaphoreType.DMA((2, n_tm)),
                pltpu.SemaphoreType.DMA((2,)),
            ],
            compiler_params=pltpu.CompilerParams(
                collective_id=0, has_side_effects=True, vmem_limit_bytes=60 * 1024 * 1024
            ),
        )(guess, source, regions, conductance, reluct)

    in_specs = (
        P("tm", None, "space", None, None),
        P("tm", None, "space", None, None),
        P("space", None, None),
        P(),
        P(),
    )
    out_specs = (P("tm", None, "space", None, None), P("tm", None, "space", None, None))
    return jax.shard_map(body, mesh=mesh, in_specs=in_specs, out_specs=out_specs, check_vma=False)
```

```python
import jax
import jax.numpy as jnp
from jax import lax
from jax.experimental import pallas as pl
from jax.experimental.pallas import tpu as pltpu
from jax.sharding import PartitionSpec as P

PICARD = 2
MESH = pl.DeviceIdType.MESH
PAD = 8


def place(index, count):
    if count % 4:
        return index
    odd_pair = lax.rem(lax.div(index, 2), 2)
    return index + odd_pair * (1 - 2 * lax.rem(index, 2))


def neighbour_sum(state, x, layers, r0, rows, halo):
    middle, lanes = pl.ds(PAD + r0, rows), state.shape[-1]
    centre = state[:, pl.ds(x + 1, layers), middle, :]
    first = state[:, pl.ds(x + 2, layers), middle, :] + state[:, pl.ds(x, layers), middle, :]
    above = state[:, pl.ds(x + 1, layers), pl.ds(PAD + r0 - 1, rows), :]
    below = state[:, pl.ds(x + 1, layers), pl.ds(PAD + r0 + 1, rows), :]
    if halo is not None:
        top, bottom, depth = halo
        row = lax.broadcasted_iota(jnp.int32, (rows, lanes), 0)

        def filled(side, values, at):
            return jnp.stack([
                jnp.stack([
                    jnp.where(
                        row == at,
                        jnp.broadcast_to(side[pl.ds(c * depth + x + i, 1), :], (rows, lanes)),
                        values[c, i],
                    )
                    for i in range(layers)
                ])
                for c in range(3)
            ])

        above = filled(top, above, 0)
        below = filled(bottom, below, rows - 1)
    flat = centre.reshape(-1, lanes)
    lane = lax.broadcasted_iota(jnp.int32, flat.shape, 1)
    left = jnp.where(lane == 0, 0.0, pltpu.roll(flat, 1, 1))
    right = jnp.where(lane == lanes - 1, 0.0, pltpu.roll(flat, lanes - 1, 1))
    third = (left + right).reshape(centre.shape)
    return centre, (first + (above + below)) + third


def fine(centre, total, known, cond, nu0):
    s = (centre[0] * centre[0] + centre[1] * centre[1]) + centre[2] * centre[2]
    one = 1.0 + s
    weight = nu0 * (one + 0.5 * s)
    below = cond * one + 6.0 * weight
    scale = pl.reciprocal(below, approx=True)
    scale = scale * (2.0 - below * scale)
    return (known * (one * scale)[None]) + (weight * scale)[None] * total


def kernel(
    n_tm, n_space,
    guess, source, regions, conductance, reluct,
    field, residual,
    home0, home1, home2, home_force, home_known, home_cond, home_nu,
    state0, state1, state2, force0, force1, known, points, res, out0,
    cond, nu0, w_old, w_sum,
    row_out, row_in,
    load_sem, home_send, home_recv, halo_send, halo_recv,
    move_send, move_recv, back_send, back_recv, store_sem,
):
    steps, _, depth, height, lanes = guess.shape
    rows = height // n_tm
    home, state = (home0, home1, home2), (state0, state1, state2)
    t, s = lax.axis_index("tm"), lax.axis_index("space")
    p = place(t, n_tm)
    lower_x, upper_x = s > 0, s < n_space - 1
    lower_y, upper_y = p > 0, p < n_tm - 1

    def wrap(i):
        return lax.rem(i + n_tm, n_tm)

    def block(index):
        return pl.ds(pl.multiple_of(place(index, n_tm) * rows, 8), rows)

    def home_block(index):
        return pl.ds(pl.multiple_of(place(index, n_tm) * rows + PAD, 8), rows)

    load_guess = pltpu.make_async_copy(
        guess.at[0], home[0].at[:, pl.ds(1, depth), pl.ds(PAD, height), :], load_sem.at[0]
    )
    load_force = pltpu.make_async_copy(source.at[1], home_force, load_sem.at[1])
    load_guess.start()
    load_force.start()

    zero_layer = jnp.zeros((3, height, lanes), jnp.float32)
    for b in range(2):
        home[b][:, 0, pl.ds(PAD, height), :] = zero_layer
        home[b][:, depth + 1, pl.ds(PAD, height), :] = zero_layer
        for r0 in (0, PAD + height):
            home[b][:, :, pl.ds(r0, PAD), :] = jnp.zeros((3, depth + 2, PAD, lanes), jnp.float32)
    for b in range(3):
        for layer in (0, depth + 1):
            state[b][:, :, layer, pl.ds(PAD, rows), :] = jnp.zeros((n_tm, 3, rows, lanes), jnp.float32)
    row_in[...] = jnp.zeros_like(row_in)

    barrier = pltpu.get_barrier_semaphore()
    for i in range(1, n_tm):
        pl.semaphore_signal(barrier, inc=1, device_id=(wrap(t + i), s), device_id_type=MESH)

    @pl.when(lower_x)
    def _():
        pl.semaphore_signal(barrier, inc=1, device_id=(t, s - 1), device_id_type=MESH)

    @pl.when(upper_x)
    def _():
        pl.semaphore_signal(barrier, inc=1, device_id=(t, s + 1), device_id_type=MESH)

    between = jnp.logical_and(lower_x, upper_x)

    @pl.when(between)
    def _():
        pl.semaphore_wait(barrier, n_tm + 1)

    @pl.when(jnp.logical_not(between))
    def _():
        pl.semaphore_wait(barrier, n_tm)

    def home_copies(b, first=None, last=None):
        view = pl.ds(PAD, height)
        first = home[b].at[:, 1, view, :] if first is None else first
        last = home[b].at[:, depth, view, :] if last is None else last
        down = pltpu.make_async_remote_copy(
            first, home[b].at[:, depth + 1, view, :], home_send.at[b, 0], home_recv.at[b, 0],
            device_id=(t, s - 1), device_id_type=MESH,
        )
        up = pltpu.make_async_remote_copy(
            last, home[b].at[:, 0, view, :], home_send.at[b, 1], home_recv.at[b, 1],
            device_id=(t, s + 1), device_id_type=MESH,
        )
        return down, up

    def start_pair(copies, low, high):
        @pl.when(low)
        def _():
            copies[0].start()

        @pl.when(high)
        def _():
            copies[1].start()

    def wait_pair(copies, low, high):
        @pl.when(low)
        def _():
            copies[0].wait_send()
            copies[1].wait_recv()

        @pl.when(high)
        def _():
            copies[1].wait_send()
            copies[0].wait_recv()

    def home_edges(b):
        start_pair(home_copies(b), lower_x, upper_x)

    def home_wait(b):
        wait_pair(home_copies(b), lower_x, upper_x)

    first_edges = home_copies(0, guess.at[0, :, 0], guess.at[0, :, depth - 1])
    start_pair(first_edges, lower_x, upper_x)

    def moves(which, src, dst):
        return [
            pltpu.make_async_remote_copy(
                src(wrap(t + i)), dst(t), move_send.at[which, i], move_recv.at[which, t],
                device_id=(wrap(t + i), s), device_id_type=MESH,
            )
            for i in range(1, n_tm)
        ]

    def start_moves(which, src, dst):
        pltpu.make_async_copy(src(t), dst(t), move_recv.at[which, t]).start()
        for copy in moves(which, src, dst):
            copy.start()

    def wait_moves(which, dst, index):
        pltpu.make_async_copy(dst(index), dst(index), move_recv.at[which, index]).wait()

    def source_rows(i):
        return lambda j: source.at[i, :, :, block(j), :]

    def u_rows(j):
        return home[2].at[:, pl.ds(1, depth), home_block(j), :]

    def u_slot(j):
        return state[0].at[wrap(j + 1), :, pl.ds(1, depth), pl.ds(PAD, rows), :]

    def f0_slot(j):
        return force0.at[j]

    def f1_rows(c):
        return lambda j: source.at[1, c, :, block(j), :]

    def f1_slot(c):
        return lambda j: force1.at[j, c]

    start_moves(0, source_rows(0), f0_slot)

    def lookup(ids, table):
        value = jnp.zeros(ids.shape, jnp.float32)
        for i in range(table.shape[0]):
            value = jnp.where(ids == i, table[i], value)
        return value

    my_rows = pl.ds(pl.multiple_of(p * rows, 8), rows)

    @pl.loop(0, depth)
    def _(x):
        ids = regions[x]
        home_cond[x] = lookup(ids, conductance)
        home_nu[x] = lookup(ids, reluct)
        c = home_cond[x, my_rows, :]
        n = home_nu[x, my_rows, :]
        cond[x] = c
        nu0[x] = n
        half = c / steps
        inverse = 1.0 / (half + 6.0 * n)
        w_old[x] = half * inverse
        w_sum[x] = n * inverse

    chunk = height

    def home_sweep(b, first):
        @pl.loop(0, depth)
        def _(x):
            for r0 in range(0, height, chunk):
                cut = pl.ds(r0, chunk)
                centre, total = neighbour_sum(home[b], x, 1, r0, chunk, None)
                c, n = home_cond[pl.ds(x, 1), cut, :], home_nu[pl.ds(x, 1), cut, :]
                if first:
                    k = c[None] * centre + home_force[:, pl.ds(x, 1), cut, :]
                    home_known[:, pl.ds(x, 1), cut, :] = k
                else:
                    k = home_known[:, pl.ds(x, 1), cut, :]
                home[b + 1][:, pl.ds(x + 1, 1), pl.ds(PAD + r0, chunk), :] = fine(centre, total, k, c, n)

    load_guess.wait()
    load_force.wait()
    wait_pair(first_edges, lower_x, upper_x)
    home_sweep(0, True)
    home_edges(1)
    home_wait(1)
    home_sweep(1, False)
    start_moves(1, u_rows, u_slot)

    def halo_copies(b, k):
        view = pl.ds(PAD, rows)
        tm_low, tm_high = place(p - 1, n_tm), place(p + 1, n_tm)
        x_down = pltpu.make_async_remote_copy(
            state[b].at[k, :, 1, view, :], state[b].at[k, :, depth + 1, view, :],
            halo_send.at[b, k, 0], halo_recv.at[b, k, 0], device_id=(t, s - 1), device_id_type=MESH,
        )
        x_up = pltpu.make_async_remote_copy(
            state[b].at[k, :, depth, view, :], state[b].at[k, :, 0, view, :],
            halo_send.at[b, k, 1], halo_recv.at[b, k, 1], device_id=(t, s + 1), device_id_type=MESH,
        )
        y_down = pltpu.make_async_remote_copy(
            row_out.at[b, k, 0], row_in.at[b, k, 1],
            halo_send.at[b, k, 2], halo_recv.at[b, k, 2], device_id=(tm_low, s), device_id_type=MESH,
        )
        y_up = pltpu.make_async_remote_copy(
            row_out.at[b, k, 1], row_in.at[b, k, 0],
            halo_send.at[b, k, 3], halo_recv.at[b, k, 3], device_id=(tm_high, s), device_id_type=MESH,
        )
        return (x_down, x_up), (y_down, y_up)

    def send_halo(b, k):
        along_x, along_y = halo_copies(b, k)
        start_pair(along_y, lower_y, upper_y)
        start_pair(along_x, lower_x, upper_x)

    def wait_halo(b, k):
        along_x, along_y = halo_copies(b, k)
        wait_pair(along_y, lower_y, upper_y)
        wait_pair(along_x, lower_x, upper_x)

    layers = 4 if depth % 4 == 0 else 1

    def keep_rows(b, k, x, values):
        for c in range(3):
            for i in range(layers):
                row_out[b, k, 0, pl.ds(c * depth + x + i, 1), :] = values[c, i, 0:1, :]
                row_out[b, k, 1, pl.ds(c * depth + x + i, 1), :] = values[c, i, rows - 1:rows, :]

    def sweep(b, b_out, kind, first, shift, keep):
        @pl.loop(0, n_tm)
        def _(k):
            k_in = wrap(k - 1) if shift else k
            wait_halo(b, k_in)
            halo = (row_in.at[b, k_in, 0], row_in.at[b, k_in, 1], depth)

            @pl.loop(0, depth // layers)
            def _(step):
                x = step * layers
                cut = pl.ds(x, layers)
                centre, total = neighbour_sum(state[b].at[k_in], x, layers, 0, rows, halo)
                if kind == "coarse":
                    k_now = w_old[cut][None] * centre if first else known[k, :, cut]
                    value = k_now + w_sum[cut][None] * total
                else:
                    c, n = cond[cut], nu0[cut]
                    forces = force0 if kind == "force0" else force1
                    k_now = c[None] * centre + forces[k, :, cut] if first else known[k, :, cut]
                    value = fine(centre, total, k_now, c, n)
                if first:
                    known[k, :, cut] = k_now
                if keep == "points":
                    points[k, :, cut] = value
                elif keep == "residual":
                    value = value - points[k, :, cut]
                    res[k, :, cut] = value
                elif keep == "correction":
                    value = value + res[k, :, cut]
                elif keep == "final":
                    out0[k, :, cut] = points[k, :, cut] + (value + res[k, :, cut])
                if keep != "final":
                    state[b_out][k, :, pl.ds(x + 1, layers), pl.ds(PAD, rows), :] = value
                    keep_rows(b_out, k, x, value)

            if keep != "final":
                send_halo(b_out, k)
            if keep == "final":
                send_back(len(pieces), k)

    pieces = [(c, slice(h * (depth // 2), depth if h else depth // 2)) for h in range(2) for c in range(3)]

    def back_view(which, index):
        if which < len(pieces):
            c, cut = pieces[which]
            return residual.at[0, c, cut, block(index), :]
        return home[0].at[:, pl.ds(1, depth), home_block(index), :]

    def back_source(which, k):
        if which < len(pieces):
            c, cut = pieces[which]
            return res.at[k, c, cut]
        return out0.at[k]

    def back_copy(which, k):
        return pltpu.make_async_remote_copy(
            back_source(which, k), back_view(which, t), back_send.at[which, k], back_recv.at[which, t],
            device_id=(k, s), device_id_type=MESH,
        )

    def send_back(which, k):
        @pl.when(k == t)
        def _():
            pltpu.make_async_copy(back_source(which, k), back_view(which, t), back_recv.at[which, t]).start()

        @pl.when(k != t)
        def _():
            back_copy(which, k).start()

    def send_piece(which):
        @pl.loop(0, n_tm)
        def _(k):
            send_back(which, k)

    def wait_back(which):
        for i in range(n_tm):
            j = wrap(t + i)
            view = back_view(which, j)
            pltpu.make_async_copy(view, view, back_recv.at[which, j]).wait()
            if i:
                back_copy(which, j).wait_send()

    for i in range(n_tm):
        j = wrap(t - i)
        slot = wrap(j + 1)
        wait_moves(1, u_slot, j)

        @pl.loop(0, depth // layers)
        def _(step):
            x = step * layers
            keep_rows(0, slot, x, state[0][slot, :, pl.ds(x + 1, layers), pl.ds(PAD, rows), :])

        send_halo(0, slot)

    start_moves(2, f1_rows(0), f1_slot(0))
    for j in range(n_tm):
        wait_moves(0, f0_slot, j)
    sweep(0, 1, "force0", True, False, None)
    start_moves(3, f1_rows(1), f1_slot(1))
    start_moves(4, f1_rows(2), f1_slot(2))
    sweep(1, 2, "force0", False, False, "points")
    for c in range(3):
        for j in range(n_tm):
            wait_moves(2 + c, f1_slot(c), j)
    sweep(2, 0, "force1", True, False, None)
    sweep(0, 1, "force1", False, False, None)
    sweep(1, 2, "force0", True, True, None)
    sweep(2, 0, "force0", False, False, "residual")
    b, sent = 0, 0
    for k in range(1, n_tm):
        sweep(b, (b + 1) % 3, "coarse", True, True, None)
        if sent < len(pieces):
            send_piece(sent)
            sent += 1
        sweep((b + 1) % 3, (b + 2) % 3, "coarse", False, False, "final" if k == n_tm - 1 else "correction")
        if sent < len(pieces):
            send_piece(sent)
            sent += 1
        b = (b + 2) % 3
    for which in range(sent, len(pieces)):
        send_piece(which)

    for copy in moves(0, source_rows(0), f0_slot):
        copy.wait_send()
    for copy in moves(1, u_rows, u_slot):
        copy.wait_send()
    for c in range(3):
        for copy in moves(2 + c, f1_rows(c), f1_slot(c)):
            copy.wait_send()

    wait_back(len(pieces))
    home_edges(0)
    store0 = pltpu.make_async_copy(
        home[0].at[:, pl.ds(1, depth), pl.ds(PAD, height), :], field.at[0], store_sem.at[0]
    )
    store0.start()
    home_wait(0)
    home_sweep(0, True)
    home_edges(1)
    home_wait(1)
    home_sweep(1, False)
    store1 = pltpu.make_async_copy(
        home[2].at[:, pl.ds(1, depth), pl.ds(PAD, height), :], field.at[1], store_sem.at[1]
    )
    store1.start()
    for which in range(len(pieces)):
        wait_back(which)
    store0.wait()
    store1.wait()


def solution(mesh):
    n_tm, n_space = mesh.shape["tm"], mesh.shape["space"]

    def body(guess, source, regions, conductance, reluct):
        steps, comps, depth, height, lanes = guess.shape
        rows = height // n_tm
        edge_rows = -(-comps * depth // 8) * 8
        f32 = jnp.float32
        whole = (n_tm, comps, depth, rows, lanes)

        def call(*args):
            return kernel(n_tm, n_space, *args)

        return pl.pallas_call(
            call,
            out_shape=(
                jax.ShapeDtypeStruct(guess.shape, f32),
                jax.ShapeDtypeStruct((1,) + guess.shape[1:], f32),
            ),
            in_specs=[
                pl.BlockSpec(memory_space=pl.ANY),
                pl.BlockSpec(memory_space=pl.ANY),
                pl.BlockSpec(memory_space=pltpu.VMEM),
                pl.BlockSpec(memory_space=pltpu.SMEM),
                pl.BlockSpec(memory_space=pltpu.SMEM),
            ],
            out_specs=(pl.BlockSpec(memory_space=pl.ANY), pl.BlockSpec(memory_space=pl.ANY)),
            scratch_shapes=[
                pltpu.VMEM((comps, depth + 2, height + 2 * PAD, lanes), f32),
                pltpu.VMEM((comps, depth + 2, height + 2 * PAD, lanes), f32),
                pltpu.VMEM((comps, depth + 2, height + 2 * PAD, lanes), f32),
                pltpu.VMEM((comps, depth, height, lanes), f32),
                pltpu.VMEM((comps, depth, height, lanes), f32),
                pltpu.VMEM((depth, height, lanes), f32),
                pltpu.VMEM((depth, height, lanes), f32),
                pltpu.VMEM((n_tm, comps, depth + 2, rows + 2 * PAD, lanes), f32),
                pltpu.VMEM((n_tm, comps, depth + 2, rows + 2 * PAD, lanes), f32),
                pltpu.VMEM((n_tm, comps, depth + 2, rows + 2 * PAD, lanes), f32),
                pltpu.VMEM(whole, f32),
                pltpu.VMEM(whole, f32),
                pltpu.VMEM(whole, f32),
                pltpu.VMEM(whole, f32),
                pltpu.VMEM(whole, f32),
                pltpu.VMEM(whole, f32),
                pltpu.VMEM((depth, rows, lanes), f32),
                pltpu.VMEM((depth, rows, lanes), f32),
                pltpu.VMEM((depth, rows, lanes), f32),
                pltpu.VMEM((depth, rows, lanes), f32),
                pltpu.VMEM((3, n_tm, 2, edge_rows, lanes), f32),
                pltpu.VMEM((3, n_tm, 2, edge_rows, lanes), f32),
                pltpu.SemaphoreType.DMA((2,)),
                pltpu.SemaphoreType.DMA((2, 2)),
                pltpu.SemaphoreType.DMA((2, 2)),
                pltpu.SemaphoreType.DMA((3, n_tm, 4)),
                pltpu.SemaphoreType.DMA((3, n_tm, 4)),
                pltpu.SemaphoreType.DMA((5, n_tm)),
                pltpu.SemaphoreType.DMA((5, n_tm)),
                pltpu.SemaphoreType.DMA((7, n_tm)),
                pltpu.SemaphoreType.DMA((7, n_tm)),
                pltpu.SemaphoreType.DMA((2,)),
            ],
            compiler_params=pltpu.CompilerParams(
                collective_id=0, has_side_effects=True, vmem_limit_bytes=60 * 1024 * 1024
            ),
        )(guess, source, regions, conductance, reluct)

    in_specs = (
        P("tm", None, "space", None, None),
        P("tm", None, "space", None, None),
        P("space", None, None),
        P(),
        P(),
    )
    out_specs = (P("tm", None, "space", None, None), P("tm", None, "space", None, None))
    return jax.shard_map(body, mesh=mesh, in_specs=in_specs, out_specs=out_specs, check_vma=False)
```

```python
import jax
import jax.numpy as jnp
from jax import lax
from jax.experimental import pallas as pl
from jax.experimental.pallas import tpu as pltpu
from jax.sharding import PartitionSpec as P

PICARD = 2
MESH = pl.DeviceIdType.MESH
PAD = 8


def place(index, count):
    if count % 4:
        return index
    odd_pair = lax.rem(lax.div(index, 2), 2)
    return index + odd_pair * (1 - 2 * lax.rem(index, 2))


def neighbour_sum(state, x, layers, r0, rows):
    middle, lanes = pl.ds(PAD + r0, rows), state.shape[-1]
    centre = state[:, pl.ds(x + 1, layers), middle, :]
    first = state[:, pl.ds(x + 2, layers), middle, :] + state[:, pl.ds(x, layers), middle, :]
    above = state[:, pl.ds(x + 1, layers), pl.ds(PAD + r0 - 1, rows), :]
    below = state[:, pl.ds(x + 1, layers), pl.ds(PAD + r0 + 1, rows), :]
    flat = centre.reshape(-1, lanes)
    lane = lax.broadcasted_iota(jnp.int32, flat.shape, 1)
    left = jnp.where(lane == 0, 0.0, pltpu.roll(flat, 1, 1))
    right = jnp.where(lane == lanes - 1, 0.0, pltpu.roll(flat, lanes - 1, 1))
    third = (left + right).reshape(centre.shape)
    return centre, (first + (above + below)) + third


def fine(centre, total, known, cond, nu0):
    s = (centre[0] * centre[0] + centre[1] * centre[1]) + centre[2] * centre[2]
    one = 1.0 + s
    weight = nu0 * (one + 0.5 * s)
    below = cond * one + 6.0 * weight
    scale = pl.reciprocal(below, approx=True)
    scale = scale * (2.0 - below * scale)
    return (known * (one * scale)[None]) + (weight * scale)[None] * total


def kernel(
    n_tm, n_space,
    guess, source, regions, conductance, reluct,
    field, residual,
    home0, home1, home2, home_force, home_known, home_cond, home_nu,
    state0, state1, state2, force0, force1, known, points, res, out0,
    cond, nu0, w_old, w_sum,
    load_sem, home_send, home_recv, halo_send, halo_recv,
    move_send, move_recv, back_send, back_recv, store_sem,
):
    steps, _, depth, height, lanes = guess.shape
    rows = height // n_tm
    home, state = (home0, home1, home2), (state0, state1, state2)
    t, s = lax.axis_index("tm"), lax.axis_index("space")
    p = place(t, n_tm)
    lower_x, upper_x = s > 0, s < n_space - 1
    lower_y, upper_y = p > 0, p < n_tm - 1

    def wrap(i):
        return lax.rem(i + n_tm, n_tm)

    def block(index):
        return pl.ds(pl.multiple_of(place(index, n_tm) * rows, 8), rows)

    def home_block(index):
        return pl.ds(pl.multiple_of(place(index, n_tm) * rows + PAD, 8), rows)

    load_guess = pltpu.make_async_copy(
        guess.at[0], home[0].at[:, pl.ds(1, depth), pl.ds(PAD, height), :], load_sem.at[0]
    )
    load_force = pltpu.make_async_copy(source.at[1], home_force, load_sem.at[1])
    load_guess.start()
    load_force.start()

    zero_layer = jnp.zeros((3, height, lanes), jnp.float32)
    for b in range(2):
        home[b][:, 0, pl.ds(PAD, height), :] = zero_layer
        home[b][:, depth + 1, pl.ds(PAD, height), :] = zero_layer
        for r0 in (0, PAD + height):
            home[b][:, :, pl.ds(r0, PAD), :] = jnp.zeros((3, depth + 2, PAD, lanes), jnp.float32)
    for b in range(3):
        for layer in (0, depth + 1):
            state[b][:, :, layer, pl.ds(PAD, rows), :] = jnp.zeros((n_tm, 3, rows, lanes), jnp.float32)
        for row in (PAD - 1, PAD + rows):
            state[b][:, :, :, pl.ds(row, 1), :] = jnp.zeros((n_tm, 3, depth + 2, 1, lanes), jnp.float32)

    barrier = pltpu.get_barrier_semaphore()
    for i in range(1, n_tm):
        pl.semaphore_signal(barrier, inc=1, device_id=(wrap(t + i), s), device_id_type=MESH)

    @pl.when(lower_x)
    def _():
        pl.semaphore_signal(barrier, inc=1, device_id=(t, s - 1), device_id_type=MESH)

    @pl.when(upper_x)
    def _():
        pl.semaphore_signal(barrier, inc=1, device_id=(t, s + 1), device_id_type=MESH)

    between = jnp.logical_and(lower_x, upper_x)

    @pl.when(between)
    def _():
        pl.semaphore_wait(barrier, n_tm + 1)

    @pl.when(jnp.logical_not(between))
    def _():
        pl.semaphore_wait(barrier, n_tm)

    def home_copies(b, first=None, last=None):
        view = pl.ds(PAD, height)
        first = home[b].at[:, 1, view, :] if first is None else first
        last = home[b].at[:, depth, view, :] if last is None else last
        down = pltpu.make_async_remote_copy(
            first, home[b].at[:, depth + 1, view, :], home_send.at[b, 0], home_recv.at[b, 0],
            device_id=(t, s - 1), device_id_type=MESH,
        )
        up = pltpu.make_async_remote_copy(
            last, home[b].at[:, 0, view, :], home_send.at[b, 1], home_recv.at[b, 1],
            device_id=(t, s + 1), device_id_type=MESH,
        )
        return down, up

    def start_pair(copies, low, high):
        @pl.when(low)
        def _():
            copies[0].start()

        @pl.when(high)
        def _():
            copies[1].start()

    def wait_pair(copies, low, high):
        @pl.when(low)
        def _():
            copies[0].wait_send()
            copies[1].wait_recv()

        @pl.when(high)
        def _():
            copies[1].wait_send()
            copies[0].wait_recv()

    def home_edges(b):
        start_pair(home_copies(b), lower_x, upper_x)

    def home_wait(b):
        wait_pair(home_copies(b), lower_x, upper_x)

    first_edges = home_copies(0, guess.at[0, :, 0], guess.at[0, :, depth - 1])
    start_pair(first_edges, lower_x, upper_x)

    def moves(which, src, dst):
        return [
            pltpu.make_async_remote_copy(
                src(wrap(t + i)), dst(t), move_send.at[which, i], move_recv.at[which, t],
                device_id=(wrap(t + i), s), device_id_type=MESH,
            )
            for i in range(1, n_tm)
        ]

    def start_moves(which, src, dst):
        pltpu.make_async_copy(src(t), dst(t), move_recv.at[which, t]).start()
        for copy in moves(which, src, dst):
            copy.start()

    def wait_moves(which, dst, index):
        pltpu.make_async_copy(dst(index), dst(index), move_recv.at[which, index]).wait()

    def source_rows(i):
        return lambda j: source.at[i, :, :, block(j), :]

    def u_rows(j):
        return home[2].at[:, pl.ds(1, depth), home_block(j), :]

    def u_slot(j):
        return state[0].at[wrap(j + 1), :, pl.ds(1, depth), pl.ds(PAD, rows), :]

    def f0_slot(j):
        return force0.at[j]

    def f1_rows(c):
        return lambda j: source.at[1, c, :, block(j), :]

    def f1_slot(c):
        return lambda j: force1.at[j, c]

    start_moves(0, source_rows(0), f0_slot)

    def lookup(ids, table):
        value = jnp.zeros(ids.shape, jnp.float32)
        for i in range(table.shape[0]):
            value = jnp.where(ids == i, table[i], value)
        return value

    my_rows = pl.ds(pl.multiple_of(p * rows, 8), rows)

    @pl.loop(0, depth)
    def _(x):
        ids = regions[x]
        home_cond[x] = lookup(ids, conductance)
        home_nu[x] = lookup(ids, reluct)
        c = home_cond[x, my_rows, :]
        n = home_nu[x, my_rows, :]
        cond[x] = c
        nu0[x] = n
        half = c / steps
        inverse = 1.0 / (half + 6.0 * n)
        w_old[x] = half * inverse
        w_sum[x] = n * inverse

    chunk = height

    def home_sweep(b, first):
        @pl.loop(0, depth)
        def _(x):
            for r0 in range(0, height, chunk):
                cut = pl.ds(r0, chunk)
                centre, total = neighbour_sum(home[b], x, 1, r0, chunk)
                c, n = home_cond[pl.ds(x, 1), cut, :], home_nu[pl.ds(x, 1), cut, :]
                if first:
                    k = c[None] * centre + home_force[:, pl.ds(x, 1), cut, :]
                    home_known[:, pl.ds(x, 1), cut, :] = k
                else:
                    k = home_known[:, pl.ds(x, 1), cut, :]
                home[b + 1][:, pl.ds(x + 1, 1), pl.ds(PAD + r0, chunk), :] = fine(centre, total, k, c, n)

    load_guess.wait()
    load_force.wait()
    wait_pair(first_edges, lower_x, upper_x)
    home_sweep(0, True)
    home_edges(1)
    home_wait(1)
    home_sweep(1, False)
    start_moves(1, u_rows, u_slot)

    def halo_copies(b, k):
        view = pl.ds(PAD, rows)
        tm_low, tm_high = place(p - 1, n_tm), place(p + 1, n_tm)
        x_down = pltpu.make_async_remote_copy(
            state[b].at[k, :, 1, view, :], state[b].at[k, :, depth + 1, view, :],
            halo_send.at[b, k, 0], halo_recv.at[b, k, 0], device_id=(t, s - 1), device_id_type=MESH,
        )
        x_up = pltpu.make_async_remote_copy(
            state[b].at[k, :, depth, view, :], state[b].at[k, :, 0, view, :],
            halo_send.at[b, k, 1], halo_recv.at[b, k, 1], device_id=(t, s + 1), device_id_type=MESH,
        )
        inner = pl.ds(1, depth)
        y_down = pltpu.make_async_remote_copy(
            state[b].at[k, :, inner, pl.ds(PAD, 1), :], state[b].at[k, :, inner, pl.ds(PAD + rows, 1), :],
            halo_send.at[b, k, 2], halo_recv.at[b, k, 2], device_id=(tm_low, s), device_id_type=MESH,
        )
        y_up = pltpu.make_async_remote_copy(
            state[b].at[k, :, inner, pl.ds(PAD + rows - 1, 1), :], state[b].at[k, :, inner, pl.ds(PAD - 1, 1), :],
            halo_send.at[b, k, 3], halo_recv.at[b, k, 3], device_id=(tm_high, s), device_id_type=MESH,
        )
        return (x_down, x_up), (y_down, y_up)

    def send_halo(b, k):
        along_x, along_y = halo_copies(b, k)
        start_pair(along_y, lower_y, upper_y)
        start_pair(along_x, lower_x, upper_x)

    def wait_halo(b, k):
        along_x, along_y = halo_copies(b, k)
        wait_pair(along_y, lower_y, upper_y)
        wait_pair(along_x, lower_x, upper_x)

    layers = 4 if depth % 4 == 0 else 1

    def sweep(b, b_out, kind, first, shift, keep):
        @pl.loop(0, n_tm)
        def _(k):
            k_in = wrap(k - 1) if shift else k
            wait_halo(b, k_in)

            @pl.loop(0, depth // layers)
            def _(step):
                x = step * layers
                cut = pl.ds(x, layers)
                centre, total = neighbour_sum(state[b].at[k_in], x, layers, 0, rows)
                if kind == "coarse":
                    k_now = w_old[cut][None] * centre if first else known[k, :, cut]
                    value = k_now + w_sum[cut][None] * total
                else:
                    c, n = cond[cut], nu0[cut]
                    forces = force0 if kind == "force0" else force1
                    k_now = c[None] * centre + forces[k, :, cut] if first else known[k, :, cut]
                    value = fine(centre, total, k_now, c, n)
                if first:
                    known[k, :, cut] = k_now
                if keep == "points":
                    points[k, :, cut] = value
                elif keep == "residual":
                    value = value - points[k, :, cut]
                    res[k, :, cut] = value
                elif keep == "correction":
                    value = value + res[k, :, cut]
                elif keep == "final":
                    out0[k, :, cut] = points[k, :, cut] + (value + res[k, :, cut])
                if keep != "final":
                    state[b_out][k, :, pl.ds(x + 1, layers), pl.ds(PAD, rows), :] = value

            if keep != "final":
                send_halo(b_out, k)
            if keep == "final":
                send_back(len(pieces), k)

    pieces = [(c, slice(h * (depth // 2), depth if h else depth // 2)) for h in range(2) for c in range(3)]

    def back_view(which, index):
        if which < len(pieces):
            c, cut = pieces[which]
            return residual.at[0, c, cut, block(index), :]
        return home[0].at[:, pl.ds(1, depth), home_block(index), :]

    def back_source(which, k):
        if which < len(pieces):
            c, cut = pieces[which]
            return res.at[k, c, cut]
        return out0.at[k]

    def back_copy(which, k):
        return pltpu.make_async_remote_copy(
            back_source(which, k), back_view(which, t), back_send.at[which, k], back_recv.at[which, t],
            device_id=(k, s), device_id_type=MESH,
        )

    def send_back(which, k):
        @pl.when(k == t)
        def _():
            pltpu.make_async_copy(back_source(which, k), back_view(which, t), back_recv.at[which, t]).start()

        @pl.when(k != t)
        def _():
            back_copy(which, k).start()

    def send_piece(which):
        @pl.loop(0, n_tm)
        def _(k):
            send_back(which, k)

    def wait_back(which):
        for i in range(n_tm):
            j = wrap(t + i)
            view = back_view(which, j)
            pltpu.make_async_copy(view, view, back_recv.at[which, j]).wait()
            if i:
                back_copy(which, j).wait_send()

    for i in range(n_tm):
        j = wrap(t - i)
        slot = wrap(j + 1)
        wait_moves(1, u_slot, j)

        send_halo(0, slot)

    start_moves(2, f1_rows(0), f1_slot(0))
    for j in range(n_tm):
        wait_moves(0, f0_slot, j)
    sweep(0, 1, "force0", True, False, None)
    start_moves(3, f1_rows(1), f1_slot(1))
    start_moves(4, f1_rows(2), f1_slot(2))
    sweep(1, 2, "force0", False, False, "points")
    for c in range(3):
        for j in range(n_tm):
            wait_moves(2 + c, f1_slot(c), j)
    sweep(2, 0, "force1", True, False, None)
    sweep(0, 1, "force1", False, False, None)
    sweep(1, 2, "force0", True, True, None)
    sweep(2, 0, "force0", False, False, "residual")
    b, sent = 0, 0
    for k in range(1, n_tm):
        sweep(b, (b + 1) % 3, "coarse", True, True, None)
        if sent < len(pieces):
            send_piece(sent)
            sent += 1
        sweep((b + 1) % 3, (b + 2) % 3, "coarse", False, False, "final" if k == n_tm - 1 else "correction")
        if sent < len(pieces):
            send_piece(sent)
            sent += 1
        b = (b + 2) % 3
    for which in range(sent, len(pieces)):
        send_piece(which)

    for copy in moves(0, source_rows(0), f0_slot):
        copy.wait_send()
    for copy in moves(1, u_rows, u_slot):
        copy.wait_send()
    for c in range(3):
        for copy in moves(2 + c, f1_rows(c), f1_slot(c)):
            copy.wait_send()

    wait_back(len(pieces))
    home_edges(0)
    store0 = pltpu.make_async_copy(
        home[0].at[:, pl.ds(1, depth), pl.ds(PAD, height), :], field.at[0], store_sem.at[0]
    )
    store0.start()
    home_wait(0)
    home_sweep(0, True)
    home_edges(1)
    home_wait(1)
    home_sweep(1, False)
    store1 = pltpu.make_async_copy(
        home[2].at[:, pl.ds(1, depth), pl.ds(PAD, height), :], field.at[1], store_sem.at[1]
    )
    store1.start()
    for which in range(len(pieces)):
        wait_back(which)
    store0.wait()
    store1.wait()


def solution(mesh):
    n_tm, n_space = mesh.shape["tm"], mesh.shape["space"]

    def body(guess, source, regions, conductance, reluct):
        steps, comps, depth, height, lanes = guess.shape
        rows = height // n_tm
        f32 = jnp.float32
        whole = (n_tm, comps, depth, rows, lanes)

        def call(*args):
            return kernel(n_tm, n_space, *args)

        return pl.pallas_call(
            call,
            out_shape=(
                jax.ShapeDtypeStruct(guess.shape, f32),
                jax.ShapeDtypeStruct((1,) + guess.shape[1:], f32),
            ),
            in_specs=[
                pl.BlockSpec(memory_space=pl.ANY),
                pl.BlockSpec(memory_space=pl.ANY),
                pl.BlockSpec(memory_space=pltpu.VMEM),
                pl.BlockSpec(memory_space=pltpu.SMEM),
                pl.BlockSpec(memory_space=pltpu.SMEM),
            ],
            out_specs=(pl.BlockSpec(memory_space=pl.ANY), pl.BlockSpec(memory_space=pl.ANY)),
            scratch_shapes=[
                pltpu.VMEM((comps, depth + 2, height + 2 * PAD, lanes), f32),
                pltpu.VMEM((comps, depth + 2, height + 2 * PAD, lanes), f32),
                pltpu.VMEM((comps, depth + 2, height + 2 * PAD, lanes), f32),
                pltpu.VMEM((comps, depth, height, lanes), f32),
                pltpu.VMEM((comps, depth, height, lanes), f32),
                pltpu.VMEM((depth, height, lanes), f32),
                pltpu.VMEM((depth, height, lanes), f32),
                pltpu.VMEM((n_tm, comps, depth + 2, rows + 2 * PAD, lanes), f32),
                pltpu.VMEM((n_tm, comps, depth + 2, rows + 2 * PAD, lanes), f32),
                pltpu.VMEM((n_tm, comps, depth + 2, rows + 2 * PAD, lanes), f32),
                pltpu.VMEM(whole, f32),
                pltpu.VMEM(whole, f32),
                pltpu.VMEM(whole, f32),
                pltpu.VMEM(whole, f32),
                pltpu.VMEM(whole, f32),
                pltpu.VMEM(whole, f32),
                pltpu.VMEM((depth, rows, lanes), f32),
                pltpu.VMEM((depth, rows, lanes), f32),
                pltpu.VMEM((depth, rows, lanes), f32),
                pltpu.VMEM((depth, rows, lanes), f32),
                pltpu.SemaphoreType.DMA((2,)),
                pltpu.SemaphoreType.DMA((2, 2)),
                pltpu.SemaphoreType.DMA((2, 2)),
                pltpu.SemaphoreType.DMA((3, n_tm, 4)),
                pltpu.SemaphoreType.DMA((3, n_tm, 4)),
                pltpu.SemaphoreType.DMA((5, n_tm)),
                pltpu.SemaphoreType.DMA((5, n_tm)),
                pltpu.SemaphoreType.DMA((7, n_tm)),
                pltpu.SemaphoreType.DMA((7, n_tm)),
                pltpu.SemaphoreType.DMA((2,)),
            ],
            compiler_params=pltpu.CompilerParams(
                collective_id=0, has_side_effects=True, vmem_limit_bytes=54 * 1024 * 1024
            ),
        )(guess, source, regions, conductance, reluct)

    in_specs = (
        P("tm", None, "space", None, None),
        P("tm", None, "space", None, None),
        P("space", None, None),
        P(),
        P(),
    )
    out_specs = (P("tm", None, "space", None, None), P("tm", None, "space", None, None))
    return jax.shard_map(body, mesh=mesh, in_specs=in_specs, out_specs=out_specs, check_vma=False)
```

```python
import jax
import jax.numpy as jnp
from jax import lax
from jax.experimental import pallas as pl
from jax.experimental.pallas import tpu as pltpu
from jax.sharding import PartitionSpec as P

PICARD = 2
MESH = pl.DeviceIdType.MESH
BESIDE_COARSE = 2
PAD = 8


def place(index, count):
    if count % 4:
        return index
    odd_pair = lax.rem(lax.div(index, 2), 2)
    return index + odd_pair * (1 - 2 * lax.rem(index, 2))


def neighbour_sum(state, x, layers, r0, rows):
    middle, lanes = pl.ds(PAD + r0, rows), state.shape[-1]
    centre = state[:, pl.ds(x + 1, layers), middle, :]
    first = state[:, pl.ds(x + 2, layers), middle, :] + state[:, pl.ds(x, layers), middle, :]
    above = state[:, pl.ds(x + 1, layers), pl.ds(PAD + r0 - 1, rows), :]
    below = state[:, pl.ds(x + 1, layers), pl.ds(PAD + r0 + 1, rows), :]
    flat = centre.reshape(-1, lanes)
    lane = lax.broadcasted_iota(jnp.int32, flat.shape, 1)
    left = jnp.where(lane == 0, 0.0, pltpu.roll(flat, 1, 1))
    right = jnp.where(lane == lanes - 1, 0.0, pltpu.roll(flat, lanes - 1, 1))
    third = (left + right).reshape(centre.shape)
    return centre, (first + (above + below)) + third


def fine(centre, total, known, cond, nu0):
    s = (centre[0] * centre[0] + centre[1] * centre[1]) + centre[2] * centre[2]
    one = 1.0 + s
    weight = nu0 * (one + 0.5 * s)
    below = cond * one + 6.0 * weight
    scale = pl.reciprocal(below, approx=True)
    scale = scale * (2.0 - below * scale)
    return (known * (one * scale)[None]) + (weight * scale)[None] * total


def kernel(
    n_tm, n_space,
    guess, source, regions, conductance, reluct,
    field, residual,
    home0, home1, home2, home_force, home_known, home_cond, home_nu,
    state0, state1, state2, force0, force1, known, points, res, out0,
    cond, nu0, w_old, w_sum,
    load_sem, home_send, home_recv, halo_send, halo_recv,
    move_send, move_recv, back_send, back_recv, store_sem,
):
    steps, _, depth, height, lanes = guess.shape
    rows = height // n_tm
    home, state = (home0, home1, home2), (state0, state1, state2)
    t, s = lax.axis_index("tm"), lax.axis_index("space")
    p = place(t, n_tm)
    lower_x, upper_x = s > 0, s < n_space - 1
    lower_y, upper_y = p > 0, p < n_tm - 1

    def wrap(i):
        return lax.rem(i + n_tm, n_tm)

    def block(index):
        return pl.ds(pl.multiple_of(place(index, n_tm) * rows, 8), rows)

    def home_block(index):
        return pl.ds(pl.multiple_of(place(index, n_tm) * rows + PAD, 8), rows)

    load_guess = pltpu.make_async_copy(
        guess.at[0], home[0].at[:, pl.ds(1, depth), pl.ds(PAD, height), :], load_sem.at[0]
    )
    load_force = pltpu.make_async_copy(source.at[1], home_force, load_sem.at[1])
    load_guess.start()
    load_force.start()

    zero_layer = jnp.zeros((3, height, lanes), jnp.float32)
    for b in range(2):
        home[b][:, 0, pl.ds(PAD, height), :] = zero_layer
        home[b][:, depth + 1, pl.ds(PAD, height), :] = zero_layer
        for r0 in (0, PAD + height):
            home[b][:, :, pl.ds(r0, PAD), :] = jnp.zeros((3, depth + 2, PAD, lanes), jnp.float32)
    for b in range(3):
        for layer in (0, depth + 1):
            state[b][:, :, layer, pl.ds(PAD, rows), :] = jnp.zeros((n_tm, 3, rows, lanes), jnp.float32)
        for row in (PAD - 1, PAD + rows):
            state[b][:, :, :, pl.ds(row, 1), :] = jnp.zeros((n_tm, 3, depth + 2, 1, lanes), jnp.float32)

    barrier = pltpu.get_barrier_semaphore()
    for i in range(1, n_tm):
        pl.semaphore_signal(barrier, inc=1, device_id=(wrap(t + i), s), device_id_type=MESH)

    @pl.when(lower_x)
    def _():
        pl.semaphore_signal(barrier, inc=1, device_id=(t, s - 1), device_id_type=MESH)

    @pl.when(upper_x)
    def _():
        pl.semaphore_signal(barrier, inc=1, device_id=(t, s + 1), device_id_type=MESH)

    between = jnp.logical_and(lower_x, upper_x)

    @pl.when(between)
    def _():
        pl.semaphore_wait(barrier, n_tm + 1)

    @pl.when(jnp.logical_not(between))
    def _():
        pl.semaphore_wait(barrier, n_tm)

    def home_copies(b, first=None, last=None):
        view = pl.ds(PAD, height)
        first = home[b].at[:, 1, view, :] if first is None else first
        last = home[b].at[:, depth, view, :] if last is None else last
        down = pltpu.make_async_remote_copy(
            first, home[b].at[:, depth + 1, view, :], home_send.at[b, 0], home_recv.at[b, 0],
            device_id=(t, s - 1), device_id_type=MESH,
        )
        up = pltpu.make_async_remote_copy(
            last, home[b].at[:, 0, view, :], home_send.at[b, 1], home_recv.at[b, 1],
            device_id=(t, s + 1), device_id_type=MESH,
        )
        return down, up

    def start_pair(copies, low, high):
        @pl.when(low)
        def _():
            copies[0].start()

        @pl.when(high)
        def _():
            copies[1].start()

    def wait_pair(copies, low, high):
        @pl.when(low)
        def _():
            copies[0].wait_send()
            copies[1].wait_recv()

        @pl.when(high)
        def _():
            copies[1].wait_send()
            copies[0].wait_recv()

    def home_edges(b):
        start_pair(home_copies(b), lower_x, upper_x)

    first_edges = home_copies(0, guess.at[0, :, 0], guess.at[0, :, depth - 1])
    start_pair(first_edges, lower_x, upper_x)

    def moves(which, src, dst):
        return [
            pltpu.make_async_remote_copy(
                src(wrap(t + i)), dst(t), move_send.at[which, i], move_recv.at[which, t],
                device_id=(wrap(t + i), s), device_id_type=MESH,
            )
            for i in range(1, n_tm)
        ]

    def start_moves(which, src, dst):
        pltpu.make_async_copy(src(t), dst(t), move_recv.at[which, t]).start()
        for copy in moves(which, src, dst):
            copy.start()

    def wait_moves(which, dst, index):
        pltpu.make_async_copy(dst(index), dst(index), move_recv.at[which, index]).wait()

    def source_rows(i):
        return lambda j: source.at[i, :, :, block(j), :]

    def u_rows(j):
        return home[2].at[:, pl.ds(1, depth), home_block(j), :]

    def u_slot(j):
        return state[0].at[wrap(j + 1), :, pl.ds(1, depth), pl.ds(PAD, rows), :]

    def f0_slot(j):
        return force0.at[j]

    def f1_rows(c):
        return lambda j: source.at[1, c, :, block(j), :]

    def f1_slot(c):
        return lambda j: force1.at[j, c]

    start_moves(0, source_rows(0), f0_slot)

    def lookup(ids, table):
        value = jnp.zeros(ids.shape, jnp.float32)
        for i in range(table.shape[0]):
            value = jnp.where(ids == i, table[i], value)
        return value

    my_rows = pl.ds(pl.multiple_of(p * rows, 8), rows)

    @pl.loop(0, depth)
    def _(x):
        ids = regions[x]
        home_cond[x] = lookup(ids, conductance)
        home_nu[x] = lookup(ids, reluct)
        c = home_cond[x, my_rows, :]
        n = home_nu[x, my_rows, :]
        cond[x] = c
        nu0[x] = n
        half = c / steps
        inverse = 1.0 / (half + 6.0 * n)
        w_old[x] = half * inverse
        w_sum[x] = n * inverse

    def home_sweep(b, first, copies):
        def layer(x):
            centre, total = neighbour_sum(home[b], x, 1, 0, height)
            c, n = home_cond[pl.ds(x, 1)], home_nu[pl.ds(x, 1)]
            if first:
                k = c[None] * centre + home_force[:, pl.ds(x, 1)]
                home_known[:, pl.ds(x, 1)] = k
            else:
                k = home_known[:, pl.ds(x, 1)]
            home[b + 1][:, pl.ds(x + 1, 1), pl.ds(PAD, height), :] = fine(centre, total, k, c, n)

        @pl.loop(1, depth - 1)
        def _(x):
            layer(x)

        wait_pair(copies, lower_x, upper_x)

        @pl.loop(0, 2)
        def _(i):
            layer(i * (depth - 1))

    load_guess.wait()
    load_force.wait()
    home_sweep(0, True, first_edges)
    home_edges(1)
    home_sweep(1, False, home_copies(1))
    start_moves(1, u_rows, u_slot)

    def halo_copies(b, k):
        view = pl.ds(PAD, rows)
        tm_low, tm_high = place(p - 1, n_tm), place(p + 1, n_tm)
        x_down = pltpu.make_async_remote_copy(
            state[b].at[k, :, 1, view, :], state[b].at[k, :, depth + 1, view, :],
            halo_send.at[b, k, 0], halo_recv.at[b, k, 0], device_id=(t, s - 1), device_id_type=MESH,
        )
        x_up = pltpu.make_async_remote_copy(
            state[b].at[k, :, depth, view, :], state[b].at[k, :, 0, view, :],
            halo_send.at[b, k, 1], halo_recv.at[b, k, 1], device_id=(t, s + 1), device_id_type=MESH,
        )
        inner = pl.ds(1, depth)
        y_down = pltpu.make_async_remote_copy(
            state[b].at[k, :, inner, pl.ds(PAD, 1), :], state[b].at[k, :, inner, pl.ds(PAD + rows, 1), :],
            halo_send.at[b, k, 2], halo_recv.at[b, k, 2], device_id=(tm_low, s), device_id_type=MESH,
        )
        y_up = pltpu.make_async_remote_copy(
            state[b].at[k, :, inner, pl.ds(PAD + rows - 1, 1), :], state[b].at[k, :, inner, pl.ds(PAD - 1, 1), :],
            halo_send.at[b, k, 3], halo_recv.at[b, k, 3], device_id=(tm_high, s), device_id_type=MESH,
        )
        return (x_down, x_up), (y_down, y_up)

    def send_halo(b, k):
        along_x, along_y = halo_copies(b, k)
        start_pair(along_y, lower_y, upper_y)
        start_pair(along_x, lower_x, upper_x)

    def wait_halo(b, k):
        along_x, along_y = halo_copies(b, k)
        wait_pair(along_y, lower_y, upper_y)
        wait_pair(along_x, lower_x, upper_x)

    layers = 4 if depth % 4 == 0 else 1

    def sweep(b, b_out, kind, first, offset, shift, keep):
        @pl.loop(0, n_tm)
        def _(turn):
            k_in = lax.rem(turn + offset, n_tm)
            k = lax.rem(k_in + 1, n_tm) if shift else k_in
            wait_halo(b, k_in)

            @pl.loop(0, depth // layers)
            def _(step):
                x = step * layers
                cut = pl.ds(x, layers)
                centre, total = neighbour_sum(state[b].at[k_in], x, layers, 0, rows)
                if kind == "coarse":
                    k_now = w_old[cut][None] * centre if first else known[k, :, cut]
                    value = k_now + w_sum[cut][None] * total
                else:
                    c, n = cond[cut], nu0[cut]
                    forces = force0 if kind == "force0" else force1
                    k_now = c[None] * centre + forces[k, :, cut] if first else known[k, :, cut]
                    value = fine(centre, total, k_now, c, n)
                if first:
                    known[k, :, cut] = k_now
                if keep == "points":
                    points[k, :, cut] = value
                elif keep == "residual":
                    value = value - points[k, :, cut]
                    res[k, :, cut] = value
                elif keep == "correction":
                    value = value + res[k, :, cut]
                elif keep == "final":
                    out0[k, :, cut] = points[k, :, cut] + (value + res[k, :, cut])
                if keep != "final":
                    state[b_out][k, :, pl.ds(x + 1, layers), pl.ds(PAD, rows), :] = value

            if keep != "final":
                send_halo(b_out, k)
            if keep == "final":
                send_back(len(pieces), k)

    pieces = [(c, slice(h * (depth // 2), depth if h else depth // 2)) for h in range(2) for c in range(3)]

    def back_view(which, index):
        if which < len(pieces):
            c, cut = pieces[which]
            return residual.at[0, c, cut, block(index), :]
        return home[0].at[:, pl.ds(1, depth), home_block(index), :]

    def back_source(which, k):
        if which < len(pieces):
            c, cut = pieces[which]
            return res.at[k, c, cut]
        return out0.at[k]

    def back_copy(which, k):
        return pltpu.make_async_remote_copy(
            back_source(which, k), back_view(which, t), back_send.at[which, k], back_recv.at[which, t],
            device_id=(k, s), device_id_type=MESH,
        )

    def send_back(which, k):
        @pl.when(k == t)
        def _():
            pltpu.make_async_copy(back_source(which, k), back_view(which, t), back_recv.at[which, t]).start()

        @pl.when(k != t)
        def _():
            back_copy(which, k).start()

    def send_piece(which):
        @pl.loop(0, n_tm)
        def _(k):
            send_back(which, k)

    def wait_back(which):
        for i in range(n_tm):
            j = wrap(t + i)
            view = back_view(which, j)
            pltpu.make_async_copy(view, view, back_recv.at[which, j]).wait()
            if i:
                back_copy(which, j).wait_send()

    for slot in range(n_tm):
        wait_moves(1, u_slot, (slot - 1) % n_tm)
        send_halo(0, slot)

    start_moves(2, f1_rows(0), f1_slot(0))
    for j in range(n_tm):
        wait_moves(0, f0_slot, j)
    sweep(0, 1, "force0", True, 0, False, None)
    start_moves(3, f1_rows(1), f1_slot(1))
    start_moves(4, f1_rows(2), f1_slot(2))
    sweep(1, 2, "force0", False, 0, False, "points")
    for c in range(3):
        for j in range(n_tm):
            wait_moves(2 + c, f1_slot(c), j)
    sweep(2, 0, "force1", True, 0, False, None)
    sweep(0, 1, "force1", False, 0, False, None)
    sweep(1, 2, "force0", True, 0, True, None)
    sweep(2, 0, "force0", False, 1, False, "residual")
    b = 0
    for k in range(1, n_tm):
        sweep(b, (b + 1) % 3, "coarse", True, k, True, None)
        if k <= BESIDE_COARSE:
            send_piece(k - 1)
        last = k == n_tm - 1
        sweep((b + 1) % 3, (b + 2) % 3, "coarse", False, k + 1, False, "final" if last else "correction")
        b = (b + 2) % 3
    for which in range(min(BESIDE_COARSE, n_tm - 1), len(pieces)):
        send_piece(which)

    for copy in moves(0, source_rows(0), f0_slot):
        copy.wait_send()
    for copy in moves(1, u_rows, u_slot):
        copy.wait_send()
    for c in range(3):
        for copy in moves(2 + c, f1_rows(c), f1_slot(c)):
            copy.wait_send()

    wait_back(len(pieces))
    home_edges(0)
    store0 = pltpu.make_async_copy(
        home[0].at[:, pl.ds(1, depth), pl.ds(PAD, height), :], field.at[0], store_sem.at[0]
    )
    store0.start()
    home_sweep(0, True, home_copies(0))
    home_edges(1)
    home_sweep(1, False, home_copies(1))
    store1 = pltpu.make_async_copy(
        home[2].at[:, pl.ds(1, depth), pl.ds(PAD, height), :], field.at[1], store_sem.at[1]
    )
    store1.start()
    for which in range(len(pieces)):
        wait_back(which)
    store0.wait()
    store1.wait()


def solution(mesh):
    n_tm, n_space = mesh.shape["tm"], mesh.shape["space"]

    def body(guess, source, regions, conductance, reluct):
        steps, comps, depth, height, lanes = guess.shape
        rows = height // n_tm
        f32 = jnp.float32
        whole = (n_tm, comps, depth, rows, lanes)

        def call(*args):
            return kernel(n_tm, n_space, *args)

        return pl.pallas_call(
            call,
            out_shape=(
                jax.ShapeDtypeStruct(guess.shape, f32),
                jax.ShapeDtypeStruct((1,) + guess.shape[1:], f32),
            ),
            in_specs=[
                pl.BlockSpec(memory_space=pl.ANY),
                pl.BlockSpec(memory_space=pl.ANY),
                pl.BlockSpec(memory_space=pltpu.VMEM),
                pl.BlockSpec(memory_space=pltpu.SMEM),
                pl.BlockSpec(memory_space=pltpu.SMEM),
            ],
            out_specs=(pl.BlockSpec(memory_space=pl.ANY), pl.BlockSpec(memory_space=pl.ANY)),
            scratch_shapes=[
                pltpu.VMEM((comps, depth + 2, height + 2 * PAD, lanes), f32),
                pltpu.VMEM((comps, depth + 2, height + 2 * PAD, lanes), f32),
                pltpu.VMEM((comps, depth + 2, height + 2 * PAD, lanes), f32),
                pltpu.VMEM((comps, depth, height, lanes), f32),
                pltpu.VMEM((comps, depth, height, lanes), f32),
                pltpu.VMEM((depth, height, lanes), f32),
                pltpu.VMEM((depth, height, lanes), f32),
                pltpu.VMEM((n_tm, comps, depth + 2, rows + 2 * PAD, lanes), f32),
                pltpu.VMEM((n_tm, comps, depth + 2, rows + 2 * PAD, lanes), f32),
                pltpu.VMEM((n_tm, comps, depth + 2, rows + 2 * PAD, lanes), f32),
                pltpu.VMEM(whole, f32),
                pltpu.VMEM(whole, f32),
                pltpu.VMEM(whole, f32),
                pltpu.VMEM(whole, f32),
                pltpu.VMEM(whole, f32),
                pltpu.VMEM(whole, f32),
                pltpu.VMEM((depth, rows, lanes), f32),
                pltpu.VMEM((depth, rows, lanes), f32),
                pltpu.VMEM((depth, rows, lanes), f32),
                pltpu.VMEM((depth, rows, lanes), f32),
                pltpu.SemaphoreType.DMA((2,)),
                pltpu.SemaphoreType.DMA((2, 2)),
                pltpu.SemaphoreType.DMA((2, 2)),
                pltpu.SemaphoreType.DMA((3, n_tm, 4)),
                pltpu.SemaphoreType.DMA((3, n_tm, 4)),
                pltpu.SemaphoreType.DMA((5, n_tm)),
                pltpu.SemaphoreType.DMA((5, n_tm)),
                pltpu.SemaphoreType.DMA((7, n_tm)),
                pltpu.SemaphoreType.DMA((7, n_tm)),
                pltpu.SemaphoreType.DMA((2,)),
            ],
            compiler_params=pltpu.CompilerParams(
                collective_id=0, has_side_effects=True, vmem_limit_bytes=54 * 1024 * 1024
            ),
        )(guess, source, regions, conductance, reluct)

    in_specs = (
        P("tm", None, "space", None, None),
        P("tm", None, "space", None, None),
        P("space", None, None),
        P(),
        P(),
    )
    out_specs = (P("tm", None, "space", None, None), P("tm", None, "space", None, None))
    return jax.shard_map(body, mesh=mesh, in_specs=in_specs, out_specs=out_specs, check_vma=False)
```

```python
import jax
import jax.numpy as jnp
from jax import lax
from jax.experimental import pallas as pl
from jax.experimental.pallas import tpu as pltpu
from jax.sharding import PartitionSpec as P

PICARD = 2
MESH = pl.DeviceIdType.MESH
BESIDE_COARSE = 2
PAD = 8


def place(index, count):
    if count % 4:
        return index
    odd_pair = lax.rem(lax.div(index, 2), 2)
    return index + odd_pair * (1 - 2 * lax.rem(index, 2))


def neighbour_sum(state, x, layers, r0, rows):
    middle, lanes = pl.ds(PAD + r0, rows), state.shape[-1]
    centre = state[:, pl.ds(x + 1, layers), middle, :]
    first = state[:, pl.ds(x + 2, layers), middle, :] + state[:, pl.ds(x, layers), middle, :]
    above = state[:, pl.ds(x + 1, layers), pl.ds(PAD + r0 - 1, rows), :]
    below = state[:, pl.ds(x + 1, layers), pl.ds(PAD + r0 + 1, rows), :]
    flat = centre.reshape(-1, lanes)
    lane = lax.broadcasted_iota(jnp.int32, flat.shape, 1)
    left = jnp.where(lane == 0, 0.0, pltpu.roll(flat, 1, 1))
    right = jnp.where(lane == lanes - 1, 0.0, pltpu.roll(flat, lanes - 1, 1))
    third = (left + right).reshape(centre.shape)
    return centre, (first + (above + below)) + third


def fine(centre, total, known, cond, nu0):
    s = (centre[0] * centre[0] + centre[1] * centre[1]) + centre[2] * centre[2]
    one = 1.0 + s
    weight = nu0 * (one + 0.5 * s)
    below = cond * one + 6.0 * weight
    scale = pl.reciprocal(below, approx=True)
    scale = scale * (2.0 - below * scale)
    return (known * (one * scale)[None]) + (weight * scale)[None] * total


def kernel(
    n_tm, n_space,
    guess, source, regions, conductance, reluct,
    field, residual,
    home0, home1, home2, home_force, home_known, home_cond, home_nu,
    state0, state1, state2, force0, force1, known, points, res, out0,
    cond, nu0, w_old, w_sum,
    load_sem, home_send, home_recv, halo_send, halo_recv,
    move_send, move_recv, back_send, back_recv, store_sem,
):
    steps, _, depth, height, lanes = guess.shape
    rows = height // n_tm
    home, state = (home0, home1, home2), (state0, state1, state2)
    t, s = lax.axis_index("tm"), lax.axis_index("space")
    p = place(t, n_tm)
    lower_x, upper_x = s > 0, s < n_space - 1
    lower_y, upper_y = p > 0, p < n_tm - 1

    def wrap(i):
        return lax.rem(i + n_tm, n_tm)

    def block(index):
        return pl.ds(pl.multiple_of(place(index, n_tm) * rows, 8), rows)

    def home_block(index):
        return pl.ds(pl.multiple_of(place(index, n_tm) * rows + PAD, 8), rows)

    load_guess = pltpu.make_async_copy(
        guess.at[0], home[0].at[:, pl.ds(1, depth), pl.ds(PAD, height), :], load_sem.at[0]
    )
    load_force = pltpu.make_async_copy(source.at[1], home_force, load_sem.at[1])
    load_guess.start()
    load_force.start()

    barrier = pltpu.get_barrier_semaphore()
    for i in range(1, n_tm):
        pl.semaphore_signal(barrier, inc=1, device_id=(wrap(t + i), s), device_id_type=MESH)

    @pl.when(lower_x)
    def _():
        pl.semaphore_signal(barrier, inc=1, device_id=(t, s - 1), device_id_type=MESH)

    @pl.when(upper_x)
    def _():
        pl.semaphore_signal(barrier, inc=1, device_id=(t, s + 1), device_id_type=MESH)

    between = jnp.logical_and(lower_x, upper_x)

    @pl.when(between)
    def _():
        pl.semaphore_wait(barrier, n_tm + 1)

    @pl.when(jnp.logical_not(between))
    def _():
        pl.semaphore_wait(barrier, n_tm)

    def home_copies(b, first=None, last=None):
        view = pl.ds(PAD, height)
        first = home[b].at[:, 1, view, :] if first is None else first
        last = home[b].at[:, depth, view, :] if last is None else last
        down = pltpu.make_async_remote_copy(
            first, home[b].at[:, depth + 1, view, :], home_send.at[b, 0], home_recv.at[b, 0],
            device_id=(t, s - 1), device_id_type=MESH,
        )
        up = pltpu.make_async_remote_copy(
            last, home[b].at[:, 0, view, :], home_send.at[b, 1], home_recv.at[b, 1],
            device_id=(t, s + 1), device_id_type=MESH,
        )
        return down, up

    def start_pair(copies, low, high):
        @pl.when(low)
        def _():
            copies[0].start()

        @pl.when(high)
        def _():
            copies[1].start()

    def wait_arrived(copies, low, high):
        @pl.when(low)
        def _():
            copies[1].wait_recv()

        @pl.when(high)
        def _():
            copies[0].wait_recv()

    def wait_sent(copies, low, high):
        @pl.when(low)
        def _():
            copies[0].wait_send()

        @pl.when(high)
        def _():
            copies[1].wait_send()

    def home_edges(b):
        start_pair(home_copies(b), lower_x, upper_x)

    first_edges = home_copies(0, guess.at[0, :, 0], guess.at[0, :, depth - 1])
    start_pair(first_edges, lower_x, upper_x)

    def moves(which, src, dst):
        return [
            pltpu.make_async_remote_copy(
                src(wrap(t + i)), dst(t), move_send.at[which, i], move_recv.at[which, t],
                device_id=(wrap(t + i), s), device_id_type=MESH,
            )
            for i in range(1, n_tm)
        ]

    def start_moves(which, src, dst):
        pltpu.make_async_copy(src(t), dst(t), move_recv.at[which, t]).start()
        for copy in moves(which, src, dst):
            copy.start()

    def wait_moves(which, dst, index):
        pltpu.make_async_copy(dst(index), dst(index), move_recv.at[which, index]).wait()

    def source_rows(i):
        return lambda j: source.at[i, :, :, block(j), :]

    def u_rows(j):
        return home[2].at[:, pl.ds(1, depth), home_block(j), :]

    def u_slot(j):
        return state[0].at[wrap(j + 1), :, pl.ds(1, depth), pl.ds(PAD, rows), :]

    def f0_slot(j):
        return force0.at[j]

    def f1_rows(c):
        return lambda j: source.at[1, c, :, block(j), :]

    def f1_slot(c):
        return lambda j: force1.at[j, c]

    start_moves(0, source_rows(0), f0_slot)

    @pl.when(jnp.logical_not(lower_x))
    def _():
        for b in range(2):
            home[b][:, 0, pl.ds(PAD, height), :] = jnp.zeros((3, height, lanes), jnp.float32)
        for b in range(3):
            state[b][:, :, 0, pl.ds(PAD, rows), :] = jnp.zeros((n_tm, 3, rows, lanes), jnp.float32)

    @pl.when(jnp.logical_not(upper_x))
    def _():
        for b in range(2):
            home[b][:, depth + 1, pl.ds(PAD, height), :] = jnp.zeros((3, height, lanes), jnp.float32)
        for b in range(3):
            state[b][:, :, depth + 1, pl.ds(PAD, rows), :] = jnp.zeros((n_tm, 3, rows, lanes), jnp.float32)

    @pl.when(jnp.logical_not(lower_y))
    def _():
        for b in range(3):
            state[b][:, :, :, pl.ds(PAD - 1, 1), :] = jnp.zeros((n_tm, 3, depth + 2, 1, lanes), jnp.float32)

    @pl.when(jnp.logical_not(upper_y))
    def _():
        for b in range(3):
            state[b][:, :, :, pl.ds(PAD + rows, 1), :] = jnp.zeros((n_tm, 3, depth + 2, 1, lanes), jnp.float32)

    for b in range(2):
        for row in (PAD - 1, PAD + height):
            home[b][:, :, pl.ds(row, 1), :] = jnp.zeros((3, depth + 2, 1, lanes), jnp.float32)

    def lookup(ids, table):
        value = jnp.zeros(ids.shape, jnp.float32)
        for i in range(table.shape[0]):
            value = jnp.where(ids == i, table[i], value)
        return value

    my_rows = pl.ds(pl.multiple_of(p * rows, 8), rows)

    @pl.loop(0, depth)
    def _(x):
        ids = regions[x]
        home_cond[x] = lookup(ids, conductance)
        home_nu[x] = lookup(ids, reluct)
        c = home_cond[x, my_rows, :]
        n = home_nu[x, my_rows, :]
        cond[x] = c
        nu0[x] = n
        half = c / steps
        inverse = 1.0 / (half + 6.0 * n)
        w_old[x] = half * inverse
        w_sum[x] = n * inverse

    def home_sweep(b, first, copies):
        def layer(x):
            centre, total = neighbour_sum(home[b], x, 1, 0, height)
            c, n = home_cond[pl.ds(x, 1)], home_nu[pl.ds(x, 1)]
            if first:
                k = c[None] * centre + home_force[:, pl.ds(x, 1)]
                home_known[:, pl.ds(x, 1)] = k
            else:
                k = home_known[:, pl.ds(x, 1)]
            home[b + 1][:, pl.ds(x + 1, 1), pl.ds(PAD, height), :] = fine(centre, total, k, c, n)

        @pl.loop(1, depth - 1)
        def _(x):
            layer(x)

        wait_arrived(copies, lower_x, upper_x)

        @pl.loop(0, 2)
        def _(i):
            layer(i * (depth - 1))

        wait_sent(copies, lower_x, upper_x)

    load_guess.wait()
    load_force.wait()
    home_sweep(0, True, first_edges)
    home_edges(1)
    home_sweep(1, False, home_copies(1))
    start_moves(1, u_rows, u_slot)

    def halo_copies(b, k):
        view = pl.ds(PAD, rows)
        tm_low, tm_high = place(p - 1, n_tm), place(p + 1, n_tm)
        x_down = pltpu.make_async_remote_copy(
            state[b].at[k, :, 1, view, :], state[b].at[k, :, depth + 1, view, :],
            halo_send.at[b, k, 0], halo_recv.at[b, k, 0], device_id=(t, s - 1), device_id_type=MESH,
        )
        x_up = pltpu.make_async_remote_copy(
            state[b].at[k, :, depth, view, :], state[b].at[k, :, 0, view, :],
            halo_send.at[b, k, 1], halo_recv.at[b, k, 1], device_id=(t, s + 1), device_id_type=MESH,
        )
        inner = pl.ds(1, depth)
        y_down = pltpu.make_async_remote_copy(
            state[b].at[k, :, inner, pl.ds(PAD, 1), :], state[b].at[k, :, inner, pl.ds(PAD + rows, 1), :],
            halo_send.at[b, k, 2], halo_recv.at[b, k, 2], device_id=(tm_low, s), device_id_type=MESH,
        )
        y_up = pltpu.make_async_remote_copy(
            state[b].at[k, :, inner, pl.ds(PAD + rows - 1, 1), :], state[b].at[k, :, inner, pl.ds(PAD - 1, 1), :],
            halo_send.at[b, k, 3], halo_recv.at[b, k, 3], device_id=(tm_high, s), device_id_type=MESH,
        )
        return (x_down, x_up), (y_down, y_up)

    def send_halo(b, k):
        along_x, along_y = halo_copies(b, k)
        start_pair(along_y, lower_y, upper_y)
        start_pair(along_x, lower_x, upper_x)

    layers = 4 if depth % 4 == 0 and depth > 4 else 1

    def sweep(b, b_out, kind, first, offset, shift, keep):
        @pl.loop(0, n_tm)
        def _(turn):
            k_in = lax.rem(turn + offset, n_tm)
            k = lax.rem(k_in + 1, n_tm) if shift else k_in
            along_x, along_y = halo_copies(b, k_in)
            wait_arrived(along_y, lower_y, upper_y)

            def work(step):
                x = step * layers
                cut = pl.ds(x, layers)
                centre, total = neighbour_sum(state[b].at[k_in], x, layers, 0, rows)
                if kind == "coarse":
                    k_now = w_old[cut][None] * centre if first else known[k, :, cut]
                    value = k_now + w_sum[cut][None] * total
                else:
                    c, n = cond[cut], nu0[cut]
                    forces = force0 if kind == "force0" else force1
                    k_now = c[None] * centre + forces[k, :, cut] if first else known[k, :, cut]
                    value = fine(centre, total, k_now, c, n)
                if first:
                    known[k, :, cut] = k_now
                if keep == "points":
                    points[k, :, cut] = value
                elif keep == "residual":
                    value = value - points[k, :, cut]
                    res[k, :, cut] = value
                elif keep == "correction":
                    value = value + res[k, :, cut]
                elif keep == "final":
                    out0[k, :, cut] = points[k, :, cut] + (value + res[k, :, cut])
                if keep != "final":
                    state[b_out][k, :, pl.ds(x + 1, layers), pl.ds(PAD, rows), :] = value

            @pl.loop(1, depth // layers - 1)
            def _(step):
                work(step)

            wait_arrived(along_x, lower_x, upper_x)

            @pl.loop(0, 2)
            def _(i):
                work(i * (depth // layers - 1))

            if keep != "final":
                send_halo(b_out, k)
            wait_sent(along_y, lower_y, upper_y)
            wait_sent(along_x, lower_x, upper_x)
            if keep == "final":
                send_back(len(pieces), k)

    pieces = [(c, slice(h * (depth // 2), depth if h else depth // 2)) for h in range(2) for c in range(3)]

    def back_view(which, index):
        if which < len(pieces):
            c, cut = pieces[which]
            return residual.at[0, c, cut, block(index), :]
        return home[0].at[:, pl.ds(1, depth), home_block(index), :]

    def back_source(which, k):
        if which < len(pieces):
            c, cut = pieces[which]
            return res.at[k, c, cut]
        return out0.at[k]

    def back_copy(which, k):
        return pltpu.make_async_remote_copy(
            back_source(which, k), back_view(which, t), back_send.at[which, k], back_recv.at[which, t],
            device_id=(k, s), device_id_type=MESH,
        )

    def send_back(which, k):
        @pl.when(k == t)
        def _():
            pltpu.make_async_copy(back_source(which, k), back_view(which, t), back_recv.at[which, t]).start()

        @pl.when(k != t)
        def _():
            back_copy(which, k).start()

    def send_piece(which):
        @pl.loop(0, n_tm)
        def _(k):
            send_back(which, k)

    def wait_back(which):
        for i in range(n_tm):
            j = wrap(t + i)
            view = back_view(which, j)
            pltpu.make_async_copy(view, view, back_recv.at[which, j]).wait()
            if i:
                back_copy(which, j).wait_send()

    for slot in range(n_tm):
        wait_moves(1, u_slot, (slot - 1) % n_tm)
        send_halo(0, slot)

    start_moves(2, f1_rows(0), f1_slot(0))
    for j in range(n_tm):
        wait_moves(0, f0_slot, j)
    sweep(0, 1, "force0", True, 0, False, None)
    start_moves(3, f1_rows(1), f1_slot(1))
    start_moves(4, f1_rows(2), f1_slot(2))
    sweep(1, 2, "force0", False, 0, False, "points")
    for c in range(3):
        for j in range(n_tm):
            wait_moves(2 + c, f1_slot(c), j)
    sweep(2, 0, "force1", True, 0, False, None)
    sweep(0, 1, "force1", False, 0, False, None)
    sweep(1, 2, "force0", True, 0, True, None)
    sweep(2, 0, "force0", False, 1, False, "residual")
    b = 0
    for k in range(1, n_tm):
        sweep(b, (b + 1) % 3, "coarse", True, k, True, None)
        if k <= BESIDE_COARSE:
            send_piece(k - 1)
        last = k == n_tm - 1
        sweep((b + 1) % 3, (b + 2) % 3, "coarse", False, k + 1, False, "final" if last else "correction")
        b = (b + 2) % 3
    for which in range(min(BESIDE_COARSE, n_tm - 1), len(pieces)):
        send_piece(which)

    for copy in moves(0, source_rows(0), f0_slot):
        copy.wait_send()
    for copy in moves(1, u_rows, u_slot):
        copy.wait_send()
    for c in range(3):
        for copy in moves(2 + c, f1_rows(c), f1_slot(c)):
            copy.wait_send()

    wait_back(len(pieces))
    home_edges(0)
    store0 = pltpu.make_async_copy(
        home[0].at[:, pl.ds(1, depth), pl.ds(PAD, height), :], field.at[0], store_sem.at[0]
    )
    store0.start()
    home_sweep(0, True, home_copies(0))
    home_edges(1)
    home_sweep(1, False, home_copies(1))
    store1 = pltpu.make_async_copy(
        home[2].at[:, pl.ds(1, depth), pl.ds(PAD, height), :], field.at[1], store_sem.at[1]
    )
    store1.start()
    for which in range(len(pieces)):
        wait_back(which)
    store0.wait()
    store1.wait()


def solution(mesh):
    n_tm, n_space = mesh.shape["tm"], mesh.shape["space"]

    def body(guess, source, regions, conductance, reluct):
        steps, comps, depth, height, lanes = guess.shape
        rows = height // n_tm
        f32 = jnp.float32
        whole = (n_tm, comps, depth, rows, lanes)

        def call(*args):
            return kernel(n_tm, n_space, *args)

        return pl.pallas_call(
            call,
            out_shape=(
                jax.ShapeDtypeStruct(guess.shape, f32),
                jax.ShapeDtypeStruct((1,) + guess.shape[1:], f32),
            ),
            in_specs=[
                pl.BlockSpec(memory_space=pl.ANY),
                pl.BlockSpec(memory_space=pl.ANY),
                pl.BlockSpec(memory_space=pltpu.VMEM),
                pl.BlockSpec(memory_space=pltpu.SMEM),
                pl.BlockSpec(memory_space=pltpu.SMEM),
            ],
            out_specs=(pl.BlockSpec(memory_space=pl.ANY), pl.BlockSpec(memory_space=pl.ANY)),
            scratch_shapes=[
                pltpu.VMEM((comps, depth + 2, height + 2 * PAD, lanes), f32),
                pltpu.VMEM((comps, depth + 2, height + 2 * PAD, lanes), f32),
                pltpu.VMEM((comps, depth + 2, height + 2 * PAD, lanes), f32),
                pltpu.VMEM((comps, depth, height, lanes), f32),
                pltpu.VMEM((comps, depth, height, lanes), f32),
                pltpu.VMEM((depth, height, lanes), f32),
                pltpu.VMEM((depth, height, lanes), f32),
                pltpu.VMEM((n_tm, comps, depth + 2, rows + 2 * PAD, lanes), f32),
                pltpu.VMEM((n_tm, comps, depth + 2, rows + 2 * PAD, lanes), f32),
                pltpu.VMEM((n_tm, comps, depth + 2, rows + 2 * PAD, lanes), f32),
                pltpu.VMEM(whole, f32),
                pltpu.VMEM(whole, f32),
                pltpu.VMEM(whole, f32),
                pltpu.VMEM(whole, f32),
                pltpu.VMEM(whole, f32),
                pltpu.VMEM(whole, f32),
                pltpu.VMEM((depth, rows, lanes), f32),
                pltpu.VMEM((depth, rows, lanes), f32),
                pltpu.VMEM((depth, rows, lanes), f32),
                pltpu.VMEM((depth, rows, lanes), f32),
                pltpu.SemaphoreType.DMA((2,)),
                pltpu.SemaphoreType.DMA((2, 2)),
                pltpu.SemaphoreType.DMA((2, 2)),
                pltpu.SemaphoreType.DMA((3, n_tm, 4)),
                pltpu.SemaphoreType.DMA((3, n_tm, 4)),
                pltpu.SemaphoreType.DMA((5, n_tm)),
                pltpu.SemaphoreType.DMA((5, n_tm)),
                pltpu.SemaphoreType.DMA((7, n_tm)),
                pltpu.SemaphoreType.DMA((7, n_tm)),
                pltpu.SemaphoreType.DMA((2,)),
            ],
            compiler_params=pltpu.CompilerParams(
                collective_id=0, has_side_effects=True, vmem_limit_bytes=54 * 1024 * 1024
            ),
        )(guess, source, regions, conductance, reluct)

    in_specs = (
        P("tm", None, "space", None, None),
        P("tm", None, "space", None, None),
        P("space", None, None),
        P(),
        P(),
    )
    out_specs = (P("tm", None, "space", None, None), P("tm", None, "space", None, None))
    return jax.shard_map(body, mesh=mesh, in_specs=in_specs, out_specs=out_specs, check_vma=False)
```

```python
import jax
import jax.numpy as jnp
from jax import lax
from jax.experimental import pallas as pl
from jax.experimental.pallas import tpu as pltpu
from jax.sharding import PartitionSpec as P

PICARD = 2
MESH = pl.DeviceIdType.MESH
BESIDE_COARSE = 2
PAD = 8


def place(index, count):
    if count % 4:
        return index
    odd_pair = lax.rem(lax.div(index, 2), 2)
    return index + odd_pair * (1 - 2 * lax.rem(index, 2))


def neighbour_sum(state, x, layers, r0, rows):
    middle, lanes = pl.ds(PAD + r0, rows), state.shape[-1]
    centre = state[:, pl.ds(x + 1, layers), middle, :]
    first = state[:, pl.ds(x + 2, layers), middle, :] + state[:, pl.ds(x, layers), middle, :]
    above = state[:, pl.ds(x + 1, layers), pl.ds(PAD + r0 - 1, rows), :]
    below = state[:, pl.ds(x + 1, layers), pl.ds(PAD + r0 + 1, rows), :]
    flat = centre.reshape(-1, lanes)
    lane = lax.broadcasted_iota(jnp.int32, flat.shape, 1)
    left = jnp.where(lane == 0, 0.0, pltpu.roll(flat, 1, 1))
    right = jnp.where(lane == lanes - 1, 0.0, pltpu.roll(flat, lanes - 1, 1))
    third = (left + right).reshape(centre.shape)
    return centre, (first + (above + below)) + third


def fine(centre, total, known, cond, nu0):
    s = (centre[0] * centre[0] + centre[1] * centre[1]) + centre[2] * centre[2]
    one = 1.0 + s
    weight = nu0 * (one + 0.5 * s)
    below = cond * one + 6.0 * weight
    scale = pl.reciprocal(below, approx=True)
    scale = scale * (2.0 - below * scale)
    return (known * (one * scale)[None]) + (weight * scale)[None] * total


def kernel(
    n_tm, n_space,
    guess, source, regions, conductance, reluct,
    field, residual,
    home0, home1, home2, home_force, home_known, home_cond, home_nu,
    state0, state1, state2, force0, force1, known, points, res, out0,
    cond, nu0, w_old, w_sum,
    load_sem, home_send, home_recv, halo_send, halo_recv,
    move_send, move_recv, back_send, back_recv, store_sem,
):
    steps, _, depth, height, lanes = guess.shape
    rows = height // n_tm
    home, state = (home0, home1, home2), (state0, state1, state2)
    t, s = lax.axis_index("tm"), lax.axis_index("space")
    p = place(t, n_tm)
    lower_x, upper_x = s > 0, s < n_space - 1
    lower_y, upper_y = p > 0, p < n_tm - 1

    def wrap(i):
        return lax.rem(i + n_tm, n_tm)

    def block(index):
        return pl.ds(pl.multiple_of(place(index, n_tm) * rows, 8), rows)

    def home_block(index):
        return pl.ds(pl.multiple_of(place(index, n_tm) * rows + PAD, 8), rows)

    load_guess = pltpu.make_async_copy(
        guess.at[0], home[0].at[:, pl.ds(1, depth), pl.ds(PAD, height), :], load_sem.at[0]
    )
    load_force = pltpu.make_async_copy(source.at[1], home_force, load_sem.at[1])
    load_guess.start()
    load_force.start()

    barrier = pltpu.get_barrier_semaphore()
    for i in range(1, n_tm):
        pl.semaphore_signal(barrier, inc=1, device_id=(wrap(t + i), s), device_id_type=MESH)

    @pl.when(lower_x)
    def _():
        pl.semaphore_signal(barrier, inc=1, device_id=(t, s - 1), device_id_type=MESH)

    @pl.when(upper_x)
    def _():
        pl.semaphore_signal(barrier, inc=1, device_id=(t, s + 1), device_id_type=MESH)

    between = jnp.logical_and(lower_x, upper_x)

    @pl.when(between)
    def _():
        pl.semaphore_wait(barrier, n_tm + 1)

    @pl.when(jnp.logical_not(between))
    def _():
        pl.semaphore_wait(barrier, n_tm)

    def home_copies(b, first=None, last=None):
        view = pl.ds(PAD, height)
        first = home[b].at[:, 1, view, :] if first is None else first
        last = home[b].at[:, depth, view, :] if last is None else last
        down = pltpu.make_async_remote_copy(
            first, home[b].at[:, depth + 1, view, :], home_send.at[b, 0], home_recv.at[b, 0],
            device_id=(t, s - 1), device_id_type=MESH,
        )
        up = pltpu.make_async_remote_copy(
            last, home[b].at[:, 0, view, :], home_send.at[b, 1], home_recv.at[b, 1],
            device_id=(t, s + 1), device_id_type=MESH,
        )
        return down, up

    def start_pair(copies, low, high):
        @pl.when(low)
        def _():
            copies[0].start()

        @pl.when(high)
        def _():
            copies[1].start()

    def wait_arrived(copies, low, high):
        @pl.when(low)
        def _():
            copies[1].wait_recv()

        @pl.when(high)
        def _():
            copies[0].wait_recv()

    def wait_sent(copies, low, high):
        @pl.when(low)
        def _():
            copies[0].wait_send()

        @pl.when(high)
        def _():
            copies[1].wait_send()

    def home_edges(b):
        start_pair(home_copies(b), lower_x, upper_x)

    first_edges = home_copies(0, guess.at[0, :, 0], guess.at[0, :, depth - 1])
    start_pair(first_edges, lower_x, upper_x)

    def moves(which, src, dst):
        return [
            pltpu.make_async_remote_copy(
                src(wrap(t + i)), dst(t), move_send.at[which, i], move_recv.at[which, t],
                device_id=(wrap(t + i), s), device_id_type=MESH,
            )
            for i in range(1, n_tm)
        ]

    def start_moves(which, src, dst):
        pltpu.make_async_copy(src(t), dst(t), move_recv.at[which, t]).start()
        for copy in moves(which, src, dst):
            copy.start()

    def wait_moves(which, dst, index):
        pltpu.make_async_copy(dst(index), dst(index), move_recv.at[which, index]).wait()

    def source_rows(i):
        return lambda j: source.at[i, :, :, block(j), :]

    def u_rows(j):
        return home[2].at[:, pl.ds(1, depth), home_block(j), :]

    def u_slot(j):
        return state[0].at[wrap(j + 1), :, pl.ds(1, depth), pl.ds(PAD, rows), :]

    def f0_slot(j):
        return force0.at[j]

    def f1_rows(c):
        return lambda j: source.at[1, c, :, block(j), :]

    def f1_slot(c):
        return lambda j: force1.at[j, c]

    start_moves(0, source_rows(0), f0_slot)

    @pl.when(jnp.logical_not(lower_x))
    def _():
        for b in range(2):
            home[b][:, 0, pl.ds(PAD, height), :] = jnp.zeros((3, height, lanes), jnp.float32)
        for b in range(3):
            state[b][:, :, 0, pl.ds(PAD, rows), :] = jnp.zeros((n_tm, 3, rows, lanes), jnp.float32)

    @pl.when(jnp.logical_not(upper_x))
    def _():
        for b in range(2):
            home[b][:, depth + 1, pl.ds(PAD, height), :] = jnp.zeros((3, height, lanes), jnp.float32)
        for b in range(3):
            state[b][:, :, depth + 1, pl.ds(PAD, rows), :] = jnp.zeros((n_tm, 3, rows, lanes), jnp.float32)

    @pl.when(jnp.logical_not(lower_y))
    def _():
        for b in range(3):
            state[b][:, :, :, pl.ds(PAD - 1, 1), :] = jnp.zeros((n_tm, 3, depth + 2, 1, lanes), jnp.float32)

    @pl.when(jnp.logical_not(upper_y))
    def _():
        for b in range(3):
            state[b][:, :, :, pl.ds(PAD + rows, 1), :] = jnp.zeros((n_tm, 3, depth + 2, 1, lanes), jnp.float32)

    for b in range(2):
        for row in (PAD - 1, PAD + height):
            home[b][:, :, pl.ds(row, 1), :] = jnp.zeros((3, depth + 2, 1, lanes), jnp.float32)

    def lookup(ids, table):
        value = jnp.zeros(ids.shape, jnp.float32)
        for i in range(table.shape[0]):
            value = jnp.where(ids == i, table[i], value)
        return value

    my_rows = pl.ds(pl.multiple_of(p * rows, 8), rows)

    @pl.loop(0, depth)
    def _(x):
        ids = regions[x]
        home_cond[x] = lookup(ids, conductance)
        home_nu[x] = lookup(ids, reluct)
        c = home_cond[x, my_rows, :]
        n = home_nu[x, my_rows, :]
        cond[x] = c
        nu0[x] = n
        half = c / steps
        inverse = 1.0 / (half + 6.0 * n)
        w_old[x] = half * inverse
        w_sum[x] = n * inverse

    def home_sweep(b, first, copies):
        def layer(x):
            centre, total = neighbour_sum(home[b], x, 1, 0, height)
            c, n = home_cond[pl.ds(x, 1)], home_nu[pl.ds(x, 1)]
            if first:
                k = c[None] * centre + home_force[:, pl.ds(x, 1)]
                home_known[:, pl.ds(x, 1)] = k
            else:
                k = home_known[:, pl.ds(x, 1)]
            home[b + 1][:, pl.ds(x + 1, 1), pl.ds(PAD, height), :] = fine(centre, total, k, c, n)

        @pl.loop(1, depth - 1)
        def _(x):
            layer(x)

        wait_arrived(copies, lower_x, upper_x)

        @pl.loop(0, 2)
        def _(i):
            layer(i * (depth - 1))

        wait_sent(copies, lower_x, upper_x)

    load_guess.wait()
    load_force.wait()
    home_sweep(0, True, first_edges)
    home_edges(1)
    home_sweep(1, False, home_copies(1))
    start_moves(1, u_rows, u_slot)

    group = 2 if n_tm % 2 == 0 else 1

    def halo_copies(b, k):
        g = pl.ds(k * group, group)
        view = pl.ds(PAD, rows)
        tm_low, tm_high = place(p - 1, n_tm), place(p + 1, n_tm)
        x_down = pltpu.make_async_remote_copy(
            state[b].at[g, :, 1, view, :], state[b].at[g, :, depth + 1, view, :],
            halo_send.at[b, k, 0], halo_recv.at[b, k, 0], device_id=(t, s - 1), device_id_type=MESH,
        )
        x_up = pltpu.make_async_remote_copy(
            state[b].at[g, :, depth, view, :], state[b].at[g, :, 0, view, :],
            halo_send.at[b, k, 1], halo_recv.at[b, k, 1], device_id=(t, s + 1), device_id_type=MESH,
        )
        inner = pl.ds(1, depth)
        y_down = pltpu.make_async_remote_copy(
            state[b].at[g, :, inner, pl.ds(PAD, 1), :], state[b].at[g, :, inner, pl.ds(PAD + rows, 1), :],
            halo_send.at[b, k, 2], halo_recv.at[b, k, 2], device_id=(tm_low, s), device_id_type=MESH,
        )
        y_up = pltpu.make_async_remote_copy(
            state[b].at[g, :, inner, pl.ds(PAD + rows - 1, 1), :], state[b].at[g, :, inner, pl.ds(PAD - 1, 1), :],
            halo_send.at[b, k, 3], halo_recv.at[b, k, 3], device_id=(tm_high, s), device_id_type=MESH,
        )
        return (x_down, x_up), (y_down, y_up)

    def send_halo(b, k):
        along_x, along_y = halo_copies(b, k)
        start_pair(along_y, lower_y, upper_y)
        start_pair(along_x, lower_x, upper_x)

    layers = 4 if depth % 4 == 0 and depth > 4 else 1

    def sweep(b, b_out, kind, first, offset, keep):
        @pl.loop(0, n_tm // group)
        def _(g):
            along_x, along_y = halo_copies(b, g)

            def work(j, step):
                k = lax.rem(j + offset, n_tm)
                x = step * layers
                cut = pl.ds(x, layers)
                centre, total = neighbour_sum(state[b].at[j], x, layers, 0, rows)
                if kind == "coarse":
                    k_now = w_old[cut][None] * centre if first else known[k, :, cut]
                    value = k_now + w_sum[cut][None] * total
                else:
                    c, n = cond[cut], nu0[cut]
                    forces = force0 if kind == "force0" else force1
                    k_now = c[None] * centre + forces[k, :, cut] if first else known[k, :, cut]
                    value = fine(centre, total, k_now, c, n)
                if first:
                    known[k, :, cut] = k_now
                if keep == "points":
                    points[k, :, cut] = value
                elif keep == "residual":
                    value = value - points[k, :, cut]
                    res[k, :, cut] = value
                elif keep == "correction":
                    value = value + res[k, :, cut]
                elif keep == "final":
                    out0[k, :, cut] = points[k, :, cut] + (value + res[k, :, cut])
                if keep != "final":
                    state[b_out][j, :, pl.ds(x + 1, layers), pl.ds(PAD, rows), :] = value

            wait_arrived(along_y, lower_y, upper_y)

            @pl.loop(0, group)
            def _(i):
                @pl.loop(1, depth // layers - 1)
                def _(step):
                    work(g * group + i, step)

            wait_arrived(along_x, lower_x, upper_x)

            @pl.loop(0, group)
            def _(i):
                @pl.loop(0, 2)
                def _(end):
                    work(g * group + i, end * (depth // layers - 1))

                if keep == "final":
                    send_back(len(pieces), lax.rem(g * group + i + offset, n_tm))

            if keep != "final":
                send_halo(b_out, g)
            wait_sent(along_y, lower_y, upper_y)
            wait_sent(along_x, lower_x, upper_x)

    pieces = [(c, slice(h * (depth // 2), depth if h else depth // 2)) for h in range(2) for c in range(3)]

    def back_view(which, index):
        if which < len(pieces):
            c, cut = pieces[which]
            return residual.at[0, c, cut, block(index), :]
        return home[0].at[:, pl.ds(1, depth), home_block(index), :]

    def back_source(which, k):
        if which < len(pieces):
            c, cut = pieces[which]
            return res.at[k, c, cut]
        return out0.at[k]

    def back_copy(which, k):
        return pltpu.make_async_remote_copy(
            back_source(which, k), back_view(which, t), back_send.at[which, k], back_recv.at[which, t],
            device_id=(k, s), device_id_type=MESH,
        )

    def send_back(which, k):
        @pl.when(k == t)
        def _():
            pltpu.make_async_copy(back_source(which, k), back_view(which, t), back_recv.at[which, t]).start()

        @pl.when(k != t)
        def _():
            back_copy(which, k).start()

    def send_piece(which):
        @pl.loop(0, n_tm)
        def _(k):
            send_back(which, k)

    def wait_back(which):
        for i in range(n_tm):
            j = wrap(t + i)
            view = back_view(which, j)
            pltpu.make_async_copy(view, view, back_recv.at[which, j]).wait()
            if i:
                back_copy(which, j).wait_send()

    for g in range(n_tm // group):
        for slot in range(g * group, (g + 1) * group):
            wait_moves(1, u_slot, (slot - 1) % n_tm)
        send_halo(0, g)

    start_moves(2, f1_rows(0), f1_slot(0))
    for j in range(n_tm):
        wait_moves(0, f0_slot, j)
    sweep(0, 1, "force0", True, 0, None)
    start_moves(3, f1_rows(1), f1_slot(1))
    start_moves(4, f1_rows(2), f1_slot(2))
    sweep(1, 2, "force0", False, 0, "points")
    for c in range(3):
        for j in range(n_tm):
            wait_moves(2 + c, f1_slot(c), j)
    sweep(2, 0, "force1", True, 0, None)
    sweep(0, 1, "force1", False, 0, None)
    sweep(1, 2, "force0", True, 1, None)
    sweep(2, 0, "force0", False, 1, "residual")
    b = 0
    for k in range(1, n_tm):
        sweep(b, (b + 1) % 3, "coarse", True, k + 1, None)
        if k <= BESIDE_COARSE:
            send_piece(k - 1)
        last = k == n_tm - 1
        sweep((b + 1) % 3, (b + 2) % 3, "coarse", False, k + 1, "final" if last else "correction")
        b = (b + 2) % 3
    for which in range(min(BESIDE_COARSE, n_tm - 1), len(pieces)):
        send_piece(which)

    for copy in moves(0, source_rows(0), f0_slot):
        copy.wait_send()
    for copy in moves(1, u_rows, u_slot):
        copy.wait_send()
    for c in range(3):
        for copy in moves(2 + c, f1_rows(c), f1_slot(c)):
            copy.wait_send()

    wait_back(len(pieces))
    home_edges(0)
    store0 = pltpu.make_async_copy(
        home[0].at[:, pl.ds(1, depth), pl.ds(PAD, height), :], field.at[0], store_sem.at[0]
    )
    store0.start()
    home_sweep(0, True, home_copies(0))
    home_edges(1)
    home_sweep(1, False, home_copies(1))
    store1 = pltpu.make_async_copy(
        home[2].at[:, pl.ds(1, depth), pl.ds(PAD, height), :], field.at[1], store_sem.at[1]
    )
    store1.start()
    for which in range(len(pieces)):
        wait_back(which)
    store0.wait()
    store1.wait()


def solution(mesh):
    n_tm, n_space = mesh.shape["tm"], mesh.shape["space"]

    def body(guess, source, regions, conductance, reluct):
        steps, comps, depth, height, lanes = guess.shape
        rows = height // n_tm
        f32 = jnp.float32
        whole = (n_tm, comps, depth, rows, lanes)

        def call(*args):
            return kernel(n_tm, n_space, *args)

        return pl.pallas_call(
            call,
            out_shape=(
                jax.ShapeDtypeStruct(guess.shape, f32),
                jax.ShapeDtypeStruct((1,) + guess.shape[1:], f32),
            ),
            in_specs=[
                pl.BlockSpec(memory_space=pl.ANY),
                pl.BlockSpec(memory_space=pl.ANY),
                pl.BlockSpec(memory_space=pltpu.VMEM),
                pl.BlockSpec(memory_space=pltpu.SMEM),
                pl.BlockSpec(memory_space=pltpu.SMEM),
            ],
            out_specs=(pl.BlockSpec(memory_space=pl.ANY), pl.BlockSpec(memory_space=pl.ANY)),
            scratch_shapes=[
                pltpu.VMEM((comps, depth + 2, height + 2 * PAD, lanes), f32),
                pltpu.VMEM((comps, depth + 2, height + 2 * PAD, lanes), f32),
                pltpu.VMEM((comps, depth + 2, height + 2 * PAD, lanes), f32),
                pltpu.VMEM((comps, depth, height, lanes), f32),
                pltpu.VMEM((comps, depth, height, lanes), f32),
                pltpu.VMEM((depth, height, lanes), f32),
                pltpu.VMEM((depth, height, lanes), f32),
                pltpu.VMEM((n_tm, comps, depth + 2, rows + 2 * PAD, lanes), f32),
                pltpu.VMEM((n_tm, comps, depth + 2, rows + 2 * PAD, lanes), f32),
                pltpu.VMEM((n_tm, comps, depth + 2, rows + 2 * PAD, lanes), f32),
                pltpu.VMEM(whole, f32),
                pltpu.VMEM(whole, f32),
                pltpu.VMEM(whole, f32),
                pltpu.VMEM(whole, f32),
                pltpu.VMEM(whole, f32),
                pltpu.VMEM(whole, f32),
                pltpu.VMEM((depth, rows, lanes), f32),
                pltpu.VMEM((depth, rows, lanes), f32),
                pltpu.VMEM((depth, rows, lanes), f32),
                pltpu.VMEM((depth, rows, lanes), f32),
                pltpu.SemaphoreType.DMA((2,)),
                pltpu.SemaphoreType.DMA((2, 2)),
                pltpu.SemaphoreType.DMA((2, 2)),
                pltpu.SemaphoreType.DMA((3, n_tm, 4)),
                pltpu.SemaphoreType.DMA((3, n_tm, 4)),
                pltpu.SemaphoreType.DMA((5, n_tm)),
                pltpu.SemaphoreType.DMA((5, n_tm)),
                pltpu.SemaphoreType.DMA((7, n_tm)),
                pltpu.SemaphoreType.DMA((7, n_tm)),
                pltpu.SemaphoreType.DMA((2,)),
            ],
            compiler_params=pltpu.CompilerParams(
                collective_id=0, has_side_effects=True, vmem_limit_bytes=54 * 1024 * 1024
            ),
        )(guess, source, regions, conductance, reluct)

    in_specs = (
        P("tm", None, "space", None, None),
        P("tm", None, "space", None, None),
        P("space", None, None),
        P(),
        P(),
    )
    out_specs = (P("tm", None, "space", None, None), P("tm", None, "space", None, None))
    return jax.shard_map(body, mesh=mesh, in_specs=in_specs, out_specs=out_specs, check_vma=False)
```
